32 devices in a mesh: dp: 8 (over z, core), mp: 4 (over y, x).
Axes of the slice: x: 2, y: 2, z: 4, core: 2. Of those that a mesh axis runs over, the one named last changes fastest.
Arguments:
- tokens: bfloat16 [6144, 8192], P('dp', 'mp'), may hold values from -6 to 6
- frozen_weight: bfloat16 [8192, 2048], P('mp', 'dp'), may hold values from -0.0625 to 0.0625
- adapter_down_weight: bfloat16 [8192, 1024], P(None, 'mp'), may hold values from -0.0625 to 0.0625
- adapter_up_weight: bfloat16 [2, 32, 16, 1024], P(None, 'mp'), may hold values from -1.5 to 1.5
- token_adapter_index: int32 [6144], P('dp'), may hold values from 0 to 31, as said below
Outputs:
- projected: bfloat16 [6144, 2048], P(('dp', 'mp'))
The draws below stay inside these ranges and needn't reach their ends.
Inputs may be any that keep to these rules, and one draw needn't show every extreme that they name: `token_adapter_index`: A token's owner is its adapter id divided by 8, rounded down. Of the 192 tokens of each aligned block of rows (the rows of one device's output), at most 96 have the same owner; in each run of 4 such blocks that one dp index holds, one owner has exactly 96 tokens in every block.
All inputs are finite; a program needn't handle non-finite values.
Results may differ from the reference program's by a relative error of at most 0.0055.
Values may be sent and summed in bfloat16 or wider, within the bound.
No kernel may reach another device: no remote copies, remote signals or barrier semaphores. Data moves between devices by JAX's collectives and lax.ppermute only.
A program may use at most 128 MiB of HBM per device.

```python
import jax
import jax.numpy as jnp
from jax import lax

MODEL_DIM = 8192
KEY_VALUE_WIDTH = 1024
ADAPTER_RANK = 16
A_DEV = 8
TOK_DEV = 192
CAP = 96
ADAPTER_COUNT = 32
TOKENS = 6144


def draw_token_adapter_index(key, part):
    owner_count = ADAPTER_COUNT // A_DEV
    block_total = TOKENS // TOK_DEV

    def one_block(block_number):
        group_key = jax.random.fold_in(key, 1000003 + block_number // owner_count)
        hot_owner = jax.random.randint(group_key, (), 0, owner_count).astype(jnp.int32)
        block_key = jax.random.fold_in(key, block_number)
        key_place, key_order, key_pick = jax.random.split(block_key, 3)
        spread = jnp.arange((owner_count - 1) * CAP, dtype=jnp.int32) // CAP
        other_owners = (hot_owner + 1 + spread) % owner_count
        other_owners = jax.random.permutation(key_order, other_owners)
        ordered_owners = jnp.concatenate([jnp.full((CAP,), hot_owner, jnp.int32), other_owners[:TOK_DEV - CAP]])
        placement = jax.random.permutation(key_place, TOK_DEV)
        chosen_owner = jnp.zeros((TOK_DEV,), jnp.int32).at[placement].set(ordered_owners)
        picked = jax.random.randint(key_pick, (TOK_DEV,), 0, A_DEV).astype(jnp.int32)
        return chosen_owner * A_DEV + picked
    return jax.vmap(one_block)(jnp.arange(block_total, dtype=jnp.int32)).reshape(-1).astype(jnp.int32)


def raised(drawn, key, source, target, shards_of, factor):
    owner, partner = [(jnp.arange(drawn.shape[position]) // (drawn.shape[position] // shards_of)).reshape([-1 if axis == position else 1 for axis in range(drawn.ndim)]) for position in (source, target)]
    chosen = jax.random.permutation(key, shards_of)[partner]
    strong = (owner == chosen) | (owner == (partner + shards_of // 2) % shards_of)
    return jnp.where(strong, factor * drawn, drawn)


def steps_of(key, dims, cuts, smallest, high):
    factor_of, own = 1.0, jax.random.fold_in(key, 6)
    for position, blocks in cuts:
        draws = jnp.exp(jax.random.uniform(jax.random.fold_in(own, position), (blocks,), jnp.float32, smallest / len(cuts), high / len(cuts)))
        factor_of = factor_of * jnp.repeat(draws, dims[position] // blocks).reshape([-1 if axis == position else 1 for axis in range(len(dims))])
    return factor_of


def scatter_about(own_key, shape, scale, limit, shards=(), kind=jnp.bfloat16):
    loudness = steps_of(own_key, shape, shards, -0.22, 0.18) if shards else 1.0
    array = jax.random.normal(own_key, shape, jnp.float32) * scale * loudness
    return jnp.minimum(jnp.maximum(array, -limit), limit).astype(kind)


def gaussian_with(own_key, shape, scale, most, cuts, heavy, held_as=jnp.bfloat16):
    values = scale * jax.random.normal(own_key, shape, jnp.float32)
    if cuts:
        values = values * steps_of(own_key, shape, cuts, -0.22, 0.18)
    return jnp.clip(raised(values, jax.random.fold_in(own_key, 3), *heavy), -most, most).astype(held_as)


def setup_inputs(seed: int = 0) -> dict:
    splits = jax.random.split(jax.random.key(seed), 6)
    tokens = gaussian_with(splits[0], (TOKENS, MODEL_DIM), 1.0, 6.0, ((0, 8), (1, 4)), (1, 0, 8, 2.0))
    frozen_weight = scatter_about(splits[1], (MODEL_DIM, 2 * KEY_VALUE_WIDTH), MODEL_DIM ** -0.5, 0.0625, ((0, 4), (1, 8)))
    adapter_down_weight = scatter_about(splits[2], (MODEL_DIM, ADAPTER_COUNT * 2 * ADAPTER_RANK), MODEL_DIM ** -0.5, 0.0625, ((1, 4),))
    adapter_up_weight = scatter_about(splits[3], (2, ADAPTER_COUNT, ADAPTER_RANK, KEY_VALUE_WIDTH), ADAPTER_RANK ** -0.5, 1.5, ((1, 4),))
    token_adapter_index = draw_token_adapter_index(jax.random.fold_in(splits[5], 71), 0)
    return dict(tokens=tokens, frozen_weight=frozen_weight, adapter_down_weight=adapter_down_weight, adapter_up_weight=adapter_up_weight, token_adapter_index=token_adapter_index)


ADAPTER_SCALE = 2.0


def reference(tokens, frozen_weight, adapter_down_weight, adapter_up_weight, token_adapter_index):
    base_out = jnp.dot(tokens, frozen_weight, preferred_element_type=jnp.float32)
    block_count = TOKENS // TOK_DEV
    token_blocks = tokens.reshape(block_count, TOK_DEV, MODEL_DIM)
    id_blocks = token_adapter_index.reshape(block_count, TOK_DEV)
    down_tensor = adapter_down_weight.reshape(MODEL_DIM, ADAPTER_COUNT, 2 * ADAPTER_RANK)

    def adapt_block(block_pair):
        block_rows, block_labels_list = block_pair
        down_rows = jnp.take(down_tensor, block_labels_list, axis=1).astype(jnp.float32)
        low_rank = jnp.einsum("td,dtr->tr", block_rows.astype(jnp.float32), down_rows).astype(jnp.bfloat16)
        up_weight_rows = jnp.take(adapter_up_weight, block_labels_list, axis=1).astype(jnp.float32)
        low_parts = low_rank.astype(jnp.float32).reshape(TOK_DEV, 2, ADAPTER_RANK)
        adapter_updates = jnp.einsum("tpr,ptrk->tpk", low_parts, up_weight_rows).reshape(TOK_DEV, 2 * KEY_VALUE_WIDTH)
        return (ADAPTER_SCALE * adapter_updates).astype(jnp.bfloat16)

    adapter_updates = lax.map(adapt_block, (token_blocks, id_blocks)).reshape(TOKENS, 2 * KEY_VALUE_WIDTH)
    return (base_out + adapter_updates.astype(jnp.float32)).astype(jnp.bfloat16)
```

```python
import functools

import jax
import jax.numpy as jnp
from jax import lax
from jax.experimental import pallas as pl
from jax.experimental.pallas import tpu as pltpu
from jax.sharding import PartitionSpec as P

ADAPTER_SCALE = 2.0
CORES = 2
LANES = 128
VMEM_BYTES = 40 * 1024 * 1024


def params():
    return pltpu.CompilerParams(vmem_limit_bytes=VMEM_BYTES)


def load_all(pairs, sems):
    copies = [pltpu.make_async_copy(src, dst, sems.at[n]) for n, (src, dst) in enumerate(pairs)]
    for copy in copies:
        copy.start()
    for copy in copies:
        copy.wait()


def base_kernel(peers_ref, tokens_ref, mine_ref, other_ref, *rest):
    outs, (weight, sems) = rest[:-2], rest[-2:]
    step = pl.program_id(0)
    span = mine_ref.shape[1]

    @pl.when(step == 0)
    def _():
        load_all([(mine_ref, weight.at[:, :span]), (other_ref, weight.at[:, span:])], sems)

    product = jnp.dot(tokens_ref[...], weight[...], preferred_element_type=jnp.float32)
    for number, out in enumerate(outs):

        @pl.when(step == number)
        def _(out=out):
            out[...] = product.astype(out.dtype)


def base_products(peers, tokens, mine, other, mp_count):
    group_rows, features = tokens.shape
    rows, span = group_rows // mp_count, mine.shape[1]
    types = [jnp.float32] + [jnp.bfloat16] * (mp_count - 1)
    return pl.pallas_call(
        base_kernel,
        grid_spec=pltpu.PrefetchScalarGridSpec(
            num_scalar_prefetch=1,
            grid=(mp_count,),
            in_specs=[
                pl.BlockSpec((rows, features), lambda i, peers_ref: (peers_ref[i], 0)),
                pl.BlockSpec(memory_space=pl.ANY),
                pl.BlockSpec(memory_space=pl.ANY),
            ],
            out_specs=[pl.BlockSpec((rows, 2 * span), lambda i, peers_ref: (0, 0)) for _ in types],
            scratch_shapes=[pltpu.VMEM((features, 2 * span), mine.dtype), pltpu.SemaphoreType.DMA((2,))],
        ),
        out_shape=[jax.ShapeDtypeStruct((rows, 2 * span), kind) for kind in types],
        compiler_params=params(),
        cost_estimate=pl.CostEstimate(
            flops=4 * group_rows * features * span,
            bytes_accessed=2 * group_rows * features + 4 * features * span,
            transcendentals=0,
        ),
    )(peers, tokens, mine, other)


def low_kernel(mp_count, adapters, peers_ref, core_ref, tokens_ref, ids_ref, down_ref, *rest):
    pieces = rest[: 2 * (mp_count - 1)]
    outs = rest[2 * (mp_count - 1) : -2]
    weight, sems = rest[-2:]
    step, core = pl.program_id(0), core_ref[0]
    features = tokens_ref.shape[1]
    width = down_ref.shape[1]
    half = width // 2

    @pl.when(step == 0)
    def _():
        first = pl.multiple_of(peers_ref[0] * features, features)
        pairs = [(down_ref.at[pl.ds(first, features), :], weight.at[:, :width])]
        for number, piece in enumerate(pieces):
            pairs.append((piece, weight.at[:, width + number * half : width + (number + 1) * half]))
        load_all(pairs, sems)

    product = jnp.dot(tokens_ref[...], weight[...], preferred_element_type=jnp.float32)
    ids = ids_ref[...]
    rank_pair = width // adapters
    rows = ids.shape[0]
    lane_adapter = lax.broadcasted_iota(jnp.int32, (rows, half), 1) // rank_pair
    total = jnp.zeros((rows, half), jnp.float32)
    for number in range(2 * mp_count):
        owner = peers_ref[number // 2]
        if number < 2:
            part = number
        else:
            part = core if number % 2 == 0 else 1 - core
        wanted = ids - (owner * adapters + part * (adapters // 2))
        total += jnp.where(lane_adapter == wanted, product[:, number * half : (number + 1) * half], 0.0)
    shift = half // 2
    while shift >= rank_pair:
        total = total + pltpu.roll(total, shift, 1)
        shift //= 2
    for number, out in enumerate(outs):

        @pl.when(step == number)
        def _(out=out):
            out[...] = total


def low_sums(peers, core, tokens, ids, down, pieces, mp_count, adapters):
    group_rows, features = tokens.shape
    rows, width = group_rows // mp_count, down.shape[1]
    return pl.pallas_call(
        functools.partial(low_kernel, mp_count, adapters),
        grid_spec=pltpu.PrefetchScalarGridSpec(
            num_scalar_prefetch=2,
            grid=(mp_count,),
            in_specs=[
                pl.BlockSpec((rows, features), lambda i, peers_ref, core_ref: (peers_ref[i], 0)),
                pl.BlockSpec((rows, 1), lambda i, peers_ref, core_ref: (peers_ref[i], 0)),
            ]
            + [pl.BlockSpec(memory_space=pl.ANY)] * (1 + len(pieces)),
            out_specs=[
                pl.BlockSpec((rows, width // 2), lambda i, peers_ref, core_ref: (0, 0)) for _ in range(mp_count)
            ],
            scratch_shapes=[
                pltpu.VMEM((features, mp_count * width), down.dtype),
                pltpu.SemaphoreType.DMA((1 + len(pieces),)),
            ],
        ),
        out_shape=[jax.ShapeDtypeStruct((rows, width // 2), jnp.float32)] * mp_count,
        compiler_params=params(),
        cost_estimate=pl.CostEstimate(
            flops=2 * group_rows * features * mp_count * width,
            bytes_accessed=2 * group_rows * features + 2 * features * mp_count * width,
            transcendentals=0,
        ),
    )(peers, core, tokens, ids, down, *pieces)


def delta_kernel(mp_count, adapters, rank, peers_ref, core_ref, ids_ref, up_ref, *rest):
    sums = rest[:mp_count]
    pieces = rest[mp_count : mp_count + 2 * (mp_count - 1)]
    out = rest[-1]
    core = core_ref[0]
    span = up_ref.shape[2]
    low = sums[0][...]
    for number in range(1, mp_count):
        low = low + sums[number][...]
    rows, lanes = low.shape
    ids = ids_ref[...]
    lane_block = lax.broadcasted_iota(jnp.int32, (rows, lanes), 1) // rank
    even = lane_block % 2 == 0
    key_low = jnp.where(even, low, pltpu.roll(low, rank, 1))
    value_low = jnp.where(even, pltpu.roll(low, lanes - rank, 1), low)

    def spread(values, owner):
        return jnp.where(lane_block == ids - owner * adapters, values, 0.0).astype(jnp.bfloat16)

    def times(values, weights):
        return jnp.dot(values, weights, preferred_element_type=jnp.float32)

    mine_low = jnp.where(core == 0, key_low, value_low)
    other_low = jnp.where(core == 0, value_low, key_low)
    own = peers_ref[0]
    mine = times(spread(mine_low, own), up_ref[core])
    other = times(spread(other_low, own), up_ref[1 - core])
    for number in range(1, mp_count):
        owner = peers_ref[number]
        mine += times(spread(mine_low, owner), pieces[2 * number - 2][...])
        other += times(spread(other_low, owner), pieces[2 * number - 1][...])
    mine_at = pl.multiple_of(core * span, span)
    other_at = pl.multiple_of((1 - core) * span, span)
    out[:, pl.ds(mine_at, span)] = (ADAPTER_SCALE * mine).astype(out.dtype)
    out[:, pl.ds(other_at, span)] = (ADAPTER_SCALE * other).astype(out.dtype)


def deltas_of(peers, core, ids, up, sums, pieces, adapters, rank):
    mp_count = len(sums)
    rows = sums[0].shape[0]
    span = up.shape[2]
    vmem = pl.BlockSpec(memory_space=pltpu.VMEM)
    smem = pl.BlockSpec(memory_space=pltpu.SMEM)
    return pl.pallas_call(
        functools.partial(delta_kernel, mp_count, adapters, rank),
        in_specs=[smem, smem] + [vmem] * (2 + mp_count + len(pieces)),
        out_specs=vmem,
        out_shape=jax.ShapeDtypeStruct((rows, 2 * span), jnp.bfloat16),
        compiler_params=params(),
        cost_estimate=pl.CostEstimate(
            flops=4 * rows * mp_count * adapters * rank * span,
            bytes_accessed=4 * mp_count * adapters * rank * span + 4 * rows * span,
            transcendentals=0,
        ),
    )(peers, core, ids, up, *sums, *pieces)


def finish_kernel(mp_count, columns_ref, delta_ref, *rest):
    parts = rest[:mp_count]
    out, delta, done, sems = rest[-4:]
    span = done.shape[1] // 2
    places = [pl.ds(pl.multiple_of(columns_ref[n], span), span) for n in range(2)]
    load_all([(delta_ref.at[:, places[n]], delta.at[:, n * span : (n + 1) * span]) for n in range(2)], sems)
    total = parts[0][...]
    for part in parts[1:]:
        total = total + part[...].astype(jnp.float32)
    done[...] = (total + delta[...].astype(jnp.float32)).astype(done.dtype)
    load_all([(done.at[:, n * span : (n + 1) * span], out.at[:, places[n]]) for n in range(2)], sems)


def finish(columns, delta, parts, held):
    rows, span = parts[0].shape
    vmem = pl.BlockSpec(memory_space=pltpu.VMEM)
    anywhere = pl.BlockSpec(memory_space=pl.ANY)
    operands = [columns, delta, *parts] + ([] if held is None else [held])
    return pl.pallas_call(
        functools.partial(finish_kernel, len(parts)),
        in_specs=[pl.BlockSpec(memory_space=pltpu.SMEM), anywhere]
        + [vmem] * len(parts)
        + ([] if held is None else [anywhere]),
        out_specs=anywhere,
        out_shape=jax.ShapeDtypeStruct(delta.shape, delta.dtype),
        scratch_shapes=[
            pltpu.VMEM((rows, span), delta.dtype),
            pltpu.VMEM((rows, span), delta.dtype),
            pltpu.SemaphoreType.DMA((2,)),
        ],
        input_output_aliases={} if held is None else {len(operands) - 1: 0},
        compiler_params=params(),
        cost_estimate=pl.CostEstimate(flops=4 * rows * span, bytes_accessed=12 * rows * span, transcendentals=0),
    )(*operands)


def by_plane(plane, values):
    return sum(jnp.where(plane == n, value, 0) for n, value in enumerate(values)).astype(jnp.int32)


def arrival_order(plane, planes):
    sides = (1, -1) if 2 * plane < planes else (-1, 1)
    return [
        (side, distance)
        for distance in range(1, planes)
        for side in sides
        if 0 <= plane + side * distance < planes
    ]


def local(tokens, frozen_weight, adapter_down_weight, adapter_up_weight, token_adapter_index):
    mp_count, dp_count = lax.axis_size("mp"), lax.axis_size("dp")
    position, replica = lax.axis_index("mp"), lax.axis_index("dp")
    planes = dp_count // CORES
    plane, core = replica // CORES, replica % CORES
    group_rows, features = tokens.shape
    rows = group_rows // mp_count
    width = frozen_weight.shape[1]
    chunk = min(width, LANES)
    chunks = width // chunk
    adapters, rank, span = adapter_up_weight.shape[1:]
    down_width = adapter_down_weight.shape[1]

    peers = (position ^ jnp.arange(mp_count, dtype=jnp.int32)).astype(jnp.int32)
    core_of = core.astype(jnp.int32).reshape(1)
    swap_pairs = [(n, n ^ 1) for n in range(dp_count)]

    def swap(array):
        return lax.ppermute(array, "dp", swap_pairs)

    def trade(array, number):
        return lax.ppermute(array, "mp", [(n, n ^ number) for n in range(mp_count)])

    def hop(array, side, step):
        if side > 0:
            sources = range(1, planes - step + 1)
        else:
            sources = range(step - 1, planes - 1)
        pairs = [
            (CORES * n + part, CORES * (n - side) + part) for n in sources for part in range(CORES)
        ]
        return lax.ppermute(array, "dp", pairs)

    own_chunks = [frozen_weight[:, n * chunk : (n + 1) * chunk] for n in range(chunks)]
    held = {}
    for n in range(chunks):
        for side in (1, -1):
            held[side, 1, n] = hop(own_chunks[n], side, 1)

    down_mine = []
    for number in range(1, mp_count):
        piece = lax.dynamic_slice(
            adapter_down_weight,
            (peers[number] * features, core * (down_width // 2)),
            (features, down_width // 2),
        )
        down_mine.append(trade(piece, number))
    up_flat = adapter_up_weight.reshape(2, adapters * rank, span)
    up_piece = lax.dynamic_index_in_dim(up_flat, core, 0, keepdims=False)

    def exchange(mine):
        parts = base_products(peers, tokens, mine, swap(mine), mp_count)
        return [parts[0]] + [trade(parts[number], number) for number in range(1, mp_count)]

    gathered = [(by_plane(plane, range(planes)), n, exchange(own_chunks[n])) for n in range(chunks)]

    for step in range(2, planes):
        for n in range(chunks):
            for side in (1, -1):
                held[side, step, n] = hop(held[side, step - 1, n], side, step)

    up_mine = [trade(up_piece, number) for number in range(1, mp_count)]

    down_pieces = [piece for mine in down_mine for piece in (mine, swap(mine))]
    ids = token_adapter_index.reshape(group_rows, 1)
    sums = low_sums(peers, core_of, tokens, ids, adapter_down_weight, down_pieces, mp_count, adapters)
    sums = [sums[0]] + [trade(sums[number], number) for number in range(1, mp_count)]
    up_pieces = [piece for mine in up_mine for piece in (mine, swap(mine))]
    own_ids = lax.dynamic_slice_in_dim(ids, position * rows, rows)
    delta = deltas_of(peers, core_of, own_ids, up_flat, sums, up_pieces, adapters, rank)

    orders = [arrival_order(n, planes) for n in range(planes)]
    for turn in range(planes - 1):
        wanted = [order[turn] for order in orders]
        options = sorted(set(wanted))
        choice = by_plane(plane, [options.index(item) for item in wanted])
        group = by_plane(plane, [n + side * distance for n, (side, distance) in enumerate(wanted)])
        for n in range(chunks):
            mine = held[(*options[0], n)]
            for number, option in enumerate(options[1:], 1):
                mine = jnp.where(choice == number, held[(*option, n)], mine)
            gathered.append((group, n, exchange(mine)))

    out = None
    for group, n, parts in gathered:
        first = group * (CORES * width) + n * chunk
        columns = jnp.stack([first + core * width, first + (1 - core) * width]).astype(jnp.int32)
        out = finish(columns, delta, parts, out)
    return out


def solution(mesh):
    placed = (P("dp", "mp"), P("mp", "dp"), P(None, "mp"), P(None, "mp", None, None), P("dp"))
    return jax.shard_map(
        local, mesh=mesh, in_specs=placed, out_specs=P(("dp", "mp"), None), check_vma=False
    )
```

```python
import functools

import jax
import jax.numpy as jnp
from jax import lax
from jax.experimental import pallas as pl
from jax.experimental.pallas import tpu as pltpu
from jax.sharding import PartitionSpec as P

ADAPTER_SCALE = 2.0
CORES = 2
LANES = 128
VMEM_BYTES = 60 * 1024 * 1024
ANYWHERE = pl.BlockSpec(memory_space=pl.ANY)
WHOLE = pl.BlockSpec(memory_space=pltpu.VMEM)
SCALARS = pl.BlockSpec(memory_space=pltpu.SMEM)


def params():
    return pltpu.CompilerParams(vmem_limit_bytes=VMEM_BYTES)


def cost(flops, bytes_accessed):
    return pl.CostEstimate(flops=flops, bytes_accessed=bytes_accessed, transcendentals=0)


def load_all(pairs, sems):
    copies = [pltpu.make_async_copy(src, dst, sems.at[n]) for n, (src, dst) in enumerate(pairs)]
    for copy in copies:
        copy.start()
    for copy in copies:
        copy.wait()


def base_kernel(mp_count, first, info_ref, tokens_ref, shards_ref, *rest):
    outs, (weight, block, done, own, sems) = rest[:mp_count], rest[mp_count:]
    pairs, _, span = weight.shape
    width = shards_ref.shape[2]
    rows = block.shape[1]
    each = span // width
    loads = []
    for n in range(pairs * each):
        target = weight.at[n // each, :, n % each * width : (n % each + 1) * width]
        loads.append(pltpu.make_async_copy(shards_ref.at[first + n], target, sems.at[n]))
        loads[-1].start()
    order = list(reversed(range(mp_count)))
    copies = []
    for number in order:
        place = pl.ds(pl.multiple_of((info_ref[0] ^ number) * rows, rows), rows)
        copies.append(pltpu.make_async_copy(tokens_ref.at[place, :], block.at[number], sems.at[len(loads) + number]))
        copies[-1].start()
    for load in loads:
        load.wait()
    stores = []
    for number, copy in zip(order, copies):
        copy.wait()
        target = done.at[number] if number else own
        for n in range(pairs):
            product = jnp.dot(block[number], weight[n], preferred_element_type=jnp.float32)
            target[:, n * span : (n + 1) * span] = product.astype(target.dtype)
        stores.append(pltpu.make_async_copy(target, outs[number], sems.at[len(loads) + mp_count + number]))
        stores[-1].start()
    for store in stores:
        store.wait()


def base_products(info, tokens, shards, first, count, mp_count):
    group_rows, features = tokens.shape
    rows, width = group_rows // mp_count, shards.shape[2]
    span = width * count
    wide = min(span, 2 * LANES)
    return pl.pallas_call(
        functools.partial(base_kernel, mp_count, first),
        in_specs=[SCALARS, ANYWHERE, ANYWHERE],
        out_specs=[ANYWHERE] * mp_count,
        scratch_shapes=[
            pltpu.VMEM((span // wide, features, wide), tokens.dtype),
            pltpu.VMEM((mp_count, rows, features), tokens.dtype),
            pltpu.VMEM((mp_count, rows, span), jnp.bfloat16),
            pltpu.VMEM((rows, span), jnp.float32),
            pltpu.SemaphoreType.DMA((count + 2 * mp_count,)),
        ],
        out_shape=[
            jax.ShapeDtypeStruct((rows, span), jnp.bfloat16 if number else jnp.float32) for number in range(mp_count)
        ],
        compiler_params=params(),
        cost_estimate=cost(
            2 * group_rows * features * span, 2 * (group_rows * (features + span) + features * span) + 4 * rows * span
        ),
    )(info, tokens, shards)


def low_kernel(adapters, rank_pair, info_ref, tokens_hbm, ids_ref, mine_hbm, other_hbm, out, tokens_ref, pieces, sems):
    mp_count, half, width = mine_hbm.shape
    mine_ref, other_ref = pieces.at[0], pieces.at[1]
    load_all([(tokens_hbm, tokens_ref), (mine_hbm, mine_ref), (other_hbm, other_ref)], sems)
    core = info_ref[0]
    rows = tokens_ref.shape[0] // mp_count
    lane_adapter = lax.broadcasted_iota(jnp.int32, (rows, width), 1) // rank_pair
    for block in range(mp_count):
        place = slice(block * rows, (block + 1) * rows)
        ids = ids_ref[place, :]
        parts = [
            (tokens_ref[place, pl.ds(pl.multiple_of(part * half, half), half)], ref)
            for part, ref in ((core, mine_ref), (1 - core, other_ref))
        ]
        total = jnp.zeros((rows, width), jnp.float32)
        for number in range(mp_count):
            product = sum(
                jnp.dot(values, ref[number], preferred_element_type=jnp.float32) for values, ref in parts
            )
            total += jnp.where(lane_adapter == ids - number * adapters, product, 0.0)
        while total.shape[1] > LANES:
            fold = total.shape[1] // 2
            total = total[:, :fold] + total[:, fold:]
        shift = total.shape[1] // 2
        while shift >= rank_pair:
            total = total + pltpu.roll(total, shift, 1)
            shift //= 2
        out[block] = total


def low_sums(core, tokens, ids, mine, other, adapters, rank):
    group_rows, features = tokens.shape
    mp_count, _, width = mine.shape
    rows = group_rows // mp_count
    return pl.pallas_call(
        functools.partial(low_kernel, adapters, 2 * rank),
        in_specs=[SCALARS, ANYWHERE, WHOLE, ANYWHERE, ANYWHERE],
        out_specs=WHOLE,
        out_shape=jax.ShapeDtypeStruct((mp_count, rows, min(width, LANES)), jnp.float32),
        scratch_shapes=[
            pltpu.VMEM(tokens.shape, tokens.dtype),
            pltpu.VMEM((CORES, *mine.shape), mine.dtype),
            pltpu.SemaphoreType.DMA((3,)),
        ],
        compiler_params=params(),
        cost_estimate=cost(
            2 * group_rows * features * mp_count * width, 2 * features * (group_rows + mp_count * width)
        ),
    )(core, tokens, ids, mine, other)


def delta_kernel(adapters, rank, info_ref, ids_ref, sums_ref, mine_ref, other_ref, out):
    mp_count, rows, lanes = sums_ref.shape
    core = info_ref[0]
    span = mine_ref.shape[2]
    low = sums_ref[0]
    for number in range(1, mp_count):
        low = low + sums_ref[number]
    ids = ids_ref[...]
    lane_block = lax.broadcasted_iota(jnp.int32, (rows, lanes), 1) // rank
    even = lane_block % 2 == 0
    key_low = jnp.where(even, low, pltpu.roll(low, rank, 1))
    value_low = jnp.where(even, pltpu.roll(low, lanes - rank, 1), low)
    mine_low = jnp.where(core == 0, key_low, value_low)
    other_low = jnp.where(core == 0, value_low, key_low)
    for part, values, weights in ((core, mine_low, mine_ref), (1 - core, other_low, other_ref)):
        total = jnp.zeros((rows, span), jnp.float32)
        for owner in range(mp_count):
            spread = jnp.where(lane_block == ids - owner * adapters, values, 0.0).astype(jnp.bfloat16)
            total += jnp.dot(spread, weights[owner], preferred_element_type=jnp.float32)
        out[:, pl.ds(pl.multiple_of(part * span, span), span)] = (ADAPTER_SCALE * total).astype(out.dtype)


def deltas_of(core, ids, sums, mine, other, adapters, rank):
    mp_count, rows, _ = sums.shape
    span = mine.shape[2]
    return pl.pallas_call(
        functools.partial(delta_kernel, adapters, rank),
        in_specs=[SCALARS] + [WHOLE] * 4,
        out_specs=WHOLE,
        out_shape=jax.ShapeDtypeStruct((rows, 2 * span), jnp.bfloat16),
        compiler_params=params(),
        cost_estimate=cost(4 * rows * mine.size, 4 * mine.size + 4 * sums.size + 4 * rows * span),
    )(core, ids, sums, mine, other)


def finish_kernel(mp_count, columns, delta_hbm, *rest):
    parts, (out, delta, own, others, done, sems) = rest[:mp_count], rest[-6:]
    count, _, width = done.shape
    pairs = [(parts[0], own)] + [(part, others.at[n]) for n, part in enumerate(parts[1:])]
    pairs += [(delta_hbm.at[:, columns[n] : columns[n] + width], delta.at[n]) for n in range(count)]
    load_all(pairs, sems)
    stores = []
    for place in range(count):
        span = slice(place * width, (place + 1) * width)
        total = own[:, span]
        for n in range(mp_count - 1):
            total = total + others[n, :, span].astype(jnp.float32)
        done[place] = (total + delta[place].astype(jnp.float32)).astype(done.dtype)
        target = out.at[:, columns[place] : columns[place] + width]
        stores.append(pltpu.make_async_copy(done.at[place], target, sems.at[place]))
        stores[-1].start()
    for store in stores:
        store.wait()


def finish(columns, delta, parts, held):
    rows, span = parts[0].shape
    count, mp_count = len(columns), len(parts)
    width = span // count
    operands = [delta, *parts] + ([] if held is None else [held])
    return pl.pallas_call(
        functools.partial(finish_kernel, mp_count, columns),
        in_specs=[ANYWHERE] * len(operands),
        out_specs=ANYWHERE,
        out_shape=jax.ShapeDtypeStruct(delta.shape, delta.dtype),
        scratch_shapes=[
            pltpu.VMEM((count, rows, width), delta.dtype),
            pltpu.VMEM((rows, span), jnp.float32),
            pltpu.VMEM((mp_count - 1, rows, span), delta.dtype),
            pltpu.VMEM((count, rows, width), delta.dtype),
            pltpu.SemaphoreType.DMA((mp_count + count,)),
        ],
        input_output_aliases={} if held is None else {len(operands) - 1: 0},
        compiler_params=params(),
        cost_estimate=cost(4 * rows * span, 12 * rows * span),
    )(*operands)


def local(tokens, frozen_weight, adapter_down_weight, adapter_up_weight, token_adapter_index):
    mp_count, dp_count = lax.axis_size("mp"), lax.axis_size("dp")
    position, replica = lax.axis_index("mp"), lax.axis_index("dp")
    planes = dp_count // CORES
    plane, core = replica // CORES, replica % CORES
    group_rows, features = tokens.shape
    rows = group_rows // mp_count
    width = frozen_weight.shape[1]
    adapters, rank, up_span = adapter_up_weight.shape[1:]
    core_of = core.astype(jnp.int32).reshape(1)

    def info_of(*values):
        return jnp.stack([jnp.asarray(value, jnp.int32) for value in values])

    def after(array, *others):
        return lax.optimization_barrier((array, *others))[0]

    def after_all(*arrays):
        return lax.optimization_barrier(arrays)

    def swap(array):
        return lax.ppermute(array, "dp", [(n, n ^ 1) for n in range(dp_count)])

    def trade(array):
        return lax.all_to_all(array, "mp", 0, 0)

    def pass_round(blocks):
        return [
            lax.ppermute(block, "mp", [(m, m ^ n) for m in range(mp_count)]) for n, block in enumerate(blocks, 1)
        ]

    chunk = min(width, LANES)
    gathered = [
        lax.all_gather(frozen_weight[:, n * chunk : (n + 1) * chunk], "dp") for n in range(width // chunk)
    ]

    down_halves = adapter_down_weight.reshape(mp_count, CORES, features // CORES, -1)
    down_mine = trade(lax.dynamic_index_in_dim(down_halves, core, 1, keepdims=False))
    up_flat = adapter_up_weight.reshape(2, adapters * rank, up_span)
    up_half = lax.dynamic_index_in_dim(up_flat, core, 0, keepdims=False)
    ids = token_adapter_index.reshape(group_rows, 1)
    own_ids = lax.dynamic_slice_in_dim(ids, position * rows, rows)
    down_other = swap(down_mine)
    sums = trade(low_sums(core_of, tokens, ids, down_mine, down_other, adapters, rank))
    up_mine = trade(jnp.broadcast_to(up_half, (mp_count, *up_half.shape)))
    up_other = swap(up_mine)
    delta = deltas_of(core_of, own_ids, sums, up_mine, up_other, adapters, rank)

    out = None
    pieces = 2
    count = dp_count // pieces
    info = info_of(position)
    for n, shards in enumerate(gathered):
        finished = []
        if out is not None:
            shards, out = after_all(shards, out)
        for piece in range(pieces):
            own, *sent = base_products(info, tokens, shards, piece * count, count, mp_count)
            columns = [(piece * count + m) * width + n * chunk for m in range(count)]
            finished.append((columns, [own] + pass_round(sent)))
        for columns, parts in finished:
            out = finish(columns, delta, parts, out)
    return out


def solution(mesh):
    placed = (P("dp", "mp"), P("mp", "dp"), P(None, "mp"), P(None, "mp", None, None), P("dp"))
    return jax.shard_map(
        local, mesh=mesh, in_specs=placed, out_specs=P(("dp", "mp"), None), check_vma=False
    )
```

```python
import functools

import jax
import jax.numpy as jnp
from jax import lax
from jax.experimental import pallas as pl
from jax.experimental.pallas import tpu as pltpu
from jax.sharding import PartitionSpec as P

ADAPTER_SCALE = 2.0
CORES = 2
LANES = 128
COVER = 64
VMEM_BYTES = 60 * 1024 * 1024
ANYWHERE = pl.BlockSpec(memory_space=pl.ANY)
WHOLE = pl.BlockSpec(memory_space=pltpu.VMEM)
SCALARS = pl.BlockSpec(memory_space=pltpu.SMEM)


def params():
    return pltpu.CompilerParams(vmem_limit_bytes=VMEM_BYTES)


def cost(flops, bytes_accessed):
    return pl.CostEstimate(flops=flops, bytes_accessed=bytes_accessed, transcendentals=0)


def start_all(pairs, sems):
    copies = [pltpu.make_async_copy(src, dst, sems.at[n]) for n, (src, dst) in enumerate(pairs)]
    for copy in copies:
        copy.start()
    return copies


def load_all(pairs, sems):
    for copy in start_all(pairs, sems):
        copy.wait()


def base_kernel(mp_count, count, info_ref, mine_ref, other_ref, *rest):
    choices, outs, (weight, block, done, own, sems) = rest[:count], rest[-5 - mp_count : -5], rest[-5:]
    rows = block.shape[1]
    for number, choice in enumerate(choices):

        @pl.when(info_ref[1] == number)
        def _(choice=choice):
            pltpu.make_async_copy(choice, weight, sems.at[0]).start()

    order = [(number, part) for number in reversed(range(mp_count)) for part in range(CORES)]
    copies = {}
    for number, part in order:
        place = pl.ds(pl.multiple_of((info_ref[0] ^ number) * rows, rows), rows)
        n = CORES * number + part
        source = (mine_ref, other_ref)[part].at[place, :]
        copies[n] = pltpu.make_async_copy(source, block.at[n], sems.at[1 + n])
        copies[n].start()
    pltpu.make_async_copy(choices[0], weight, sems.at[0]).wait()
    stores = []
    for number, part in order:
        n = CORES * number + part
        copies[n].wait()
        target = done.at[number] if number else own
        product = jnp.dot(block[n], weight[...], preferred_element_type=jnp.float32)
        target[part * rows : (part + 1) * rows, :] = product.astype(target.dtype)
        if part:
            stores.append(pltpu.make_async_copy(target, outs[number], sems.at[1 + CORES * mp_count + number]))
            stores[-1].start()
    for store in stores:
        store.wait()


def base_products(info, mine, other, choices, mp_count, cover, *before):
    group_rows, features = mine.shape
    rows, span = group_rows // mp_count, choices[0].shape[1]
    return pl.pallas_call(
        functools.partial(base_kernel, mp_count, len(choices)),
        in_specs=[SCALARS] + [ANYWHERE] * (2 + len(choices) + len(before)),
        out_specs=[ANYWHERE] * mp_count,
        scratch_shapes=[
            pltpu.VMEM((features, span), mine.dtype),
            pltpu.VMEM((CORES * mp_count, rows, features), mine.dtype),
            pltpu.VMEM((mp_count, CORES * rows, span), jnp.bfloat16),
            pltpu.VMEM((CORES * rows, span), jnp.float32),
            pltpu.SemaphoreType.DMA((1 + (1 + CORES) * mp_count,)),
        ],
        out_shape=[
            jax.ShapeDtypeStruct((CORES * rows, span), jnp.bfloat16 if number else jnp.float32)
            for number in range(mp_count)
        ],
        compiler_params=params(),
        cost_estimate=cost(
            cover * 2 * CORES * group_rows * features * span,
            2 * (CORES * group_rows * (features + span) + features * span),
        ),
    )(info, mine, other, *choices, *before)


def cut_down_kernel(info_ref, down_ref, out, block, sems):
    mp_count, features, lanes = block.shape
    mine = pl.ds(pl.multiple_of(info_ref[0] * lanes, lanes), lanes)
    loads = start_all(
        [(down_ref.at[n * features : (n + 1) * features, mine], block.at[n]) for n in range(mp_count)], sems
    )
    stores = []
    for n, load in enumerate(loads):
        load.wait()
        stores.append(pltpu.make_async_copy(block.at[n], out.at[n], sems.at[mp_count + n]))
        stores[-1].start()
    for store in stores:
        store.wait()


def cut_down(core, down, mp_count):
    shape = mp_count, down.shape[0] // mp_count, down.shape[1] // CORES
    return pl.pallas_call(
        cut_down_kernel,
        in_specs=[SCALARS, ANYWHERE],
        out_specs=ANYWHERE,
        out_shape=jax.ShapeDtypeStruct(shape, down.dtype),
        scratch_shapes=[pltpu.VMEM(shape, down.dtype), pltpu.SemaphoreType.DMA((2 * mp_count,))],
        compiler_params=params(),
        cost_estimate=cost(0, 2 * down.size),
    )(core, down)


def cut_up_kernel(width, info_ref, up_ref, out, block, sems):
    parts, ranks, span = up_ref.shape
    lanes = block.shape[1]
    pairs = []
    for part in range(parts):
        for place in range(0, span, CORES * width):
            for first in range(place, place + width, lanes):
                columns = pl.ds(pl.multiple_of(first + info_ref[0] * width, lanes), lanes)
                row = len(pairs) * ranks
                pairs.append((up_ref.at[part, :, columns], block.at[row : row + ranks, :]))
    load_all(pairs, sems)
    load_all([(block, out.at[n]) for n in range(out.shape[0])], sems)


def cut_up(core, up, mp_count, width, lanes):
    parts, ranks, span = up.shape
    blocks = parts * span // CORES // lanes
    return pl.pallas_call(
        functools.partial(cut_up_kernel, width),
        in_specs=[SCALARS, ANYWHERE],
        out_specs=ANYWHERE,
        out_shape=jax.ShapeDtypeStruct((mp_count, blocks * ranks, lanes), up.dtype),
        scratch_shapes=[
            pltpu.VMEM((blocks * ranks, lanes), up.dtype),
            pltpu.SemaphoreType.DMA((max(blocks, mp_count),)),
        ],
        compiler_params=params(),
        cost_estimate=cost(0, 4 * mp_count * blocks * ranks * lanes),
    )(core, up)


def low_kernel(adapters, rank_pair, info_ref, mine_ref, other_ref, ids_ref, maps_ref, *rest):
    out, block, maps, sems = rest[-4:]
    mp_count, features, lanes = maps.shape
    rows = block.shape[1]
    order = [(number, part) for number in range(mp_count) for part in range(CORES)]
    pairs = [(maps_ref.at[number, :features, :], maps.at[number]) for number in range(mp_count)]
    for number, part in order:
        pairs.append(((mine_ref, other_ref)[part].at[number * rows : (number + 1) * rows, :], block.at[CORES * number + part]))
    copies = start_all(pairs, sems)
    for copy in copies[:mp_count]:
        copy.wait()
    lane_adapter = lax.broadcasted_iota(jnp.int32, (rows, lanes), 1) // rank_pair
    groups = lanes // rank_pair
    depth = CORES * rows // groups
    lane_group = lax.broadcasted_iota(jnp.int32, (depth, lanes), 1) // rank_pair
    for number in range(mp_count):
        halves = []
        for part in range(CORES):
            n = CORES * number + part
            copies[mp_count + n].wait()
            ids = ids_ref[part, number * rows : (number + 1) * rows, :]
            total = jnp.zeros((rows, lanes), jnp.float32)
            for owner in range(0, mp_count, CORES):
                both = jnp.concatenate([maps[owner], maps[owner + 1]], axis=1)
                product = jnp.dot(block[n], both, preferred_element_type=jnp.float32)
                for m in range(CORES):
                    wanted = ids - (owner + m) * adapters - info_ref[0] * groups
                    total += jnp.where(lane_adapter == wanted, product[:, m * lanes : (m + 1) * lanes], 0.0)
            shift = lanes // 2
            while shift >= rank_pair:
                total = total + pltpu.roll(total, shift, 1)
                shift //= 2
            halves.append(total)
        both = jnp.concatenate(halves, axis=0)
        packed = jnp.zeros((depth, lanes), jnp.float32)
        for group in range(groups):
            packed += jnp.where(lane_group == group, both[group * depth : (group + 1) * depth, :], 0.0)
        out[number] = packed


def low_sums(core, mine, other, ids, maps, adapters, rank, *before):
    group_rows, features = mine.shape
    mp_count, _, lanes = maps.shape
    rows = group_rows // mp_count
    depth = CORES * rows * 2 * rank // lanes
    return pl.pallas_call(
        functools.partial(low_kernel, adapters, 2 * rank),
        in_specs=[SCALARS, ANYWHERE, ANYWHERE, WHOLE, ANYWHERE] + [ANYWHERE] * len(before),
        out_specs=WHOLE,
        out_shape=jax.ShapeDtypeStruct((mp_count, depth, lanes), jnp.float32),
        scratch_shapes=[
            pltpu.VMEM((CORES * mp_count, rows, features), mine.dtype),
            pltpu.VMEM((mp_count, features, lanes), maps.dtype),
            pltpu.SemaphoreType.DMA(((1 + CORES) * mp_count,)),
        ],
        compiler_params=params(),
        cost_estimate=cost(
            2 * CORES * group_rows * features * mp_count * lanes, 2 * features * (CORES * group_rows + mp_count * lanes)
        ),
    )(core, mine, other, ids, maps, *before)


def delta_kernel(adapters, rank, ids_ref, mine_ref, other_ref, maps_ref, out, maps, sem):
    copy = pltpu.make_async_copy(maps_ref.at[:, maps_ref.shape[1] - maps.shape[1] :, :], maps, sem)
    copy.start()
    mp_count = maps.shape[0]
    planes, rows, span = out.shape
    lanes = mine_ref.shape[2]
    rank_pair = 2 * rank
    groups = lanes // rank_pair
    depth = rows // groups
    packed = sum(mine_ref[n] for n in range(mp_count))
    packed = packed + pltpu.roll(sum(other_ref[n] for n in range(mp_count)), lanes // 2, 1)
    lane_group = lax.broadcasted_iota(jnp.int32, (depth, lanes), 1) // rank_pair
    spread = []
    for group in range(groups):
        values = jnp.where(lane_group == group, packed, 0.0)
        shift = lanes // 2
        while shift >= rank_pair:
            values = values + pltpu.roll(values, shift, 1)
            shift //= 2
        spread.append(values)
    low = jnp.concatenate(spread, axis=0)
    ids = ids_ref[...]
    lane_block = lax.broadcasted_iota(jnp.int32, (rows, lanes), 1) // rank
    even = lane_block % 2 == 0
    lows = [jnp.where(even, low, pltpu.roll(low, rank, 1)), jnp.where(even, pltpu.roll(low, lanes - rank, 1), low)]
    copy.wait()
    ranks = adapters * rank
    for part in range(2):
        spreads = [
            jnp.where(lane_block == ids - owner * adapters, lows[part], 0.0).astype(jnp.bfloat16)
            for owner in range(mp_count)
        ]
        for plane in range(part * planes // 2, (part + 1) * planes // 2):
            for piece in range(span // lanes):
                first = (plane * (span // lanes) + piece) * ranks
                total = jnp.zeros((rows, lanes), jnp.float32)
                for owner in range(mp_count):
                    weights = maps[owner, first : first + ranks, :]
                    total += jnp.dot(spreads[owner], weights, preferred_element_type=jnp.float32)
                out[plane, :, piece * lanes : (piece + 1) * lanes] = (ADAPTER_SCALE * total).astype(out.dtype)


def deltas_of(ids, mine, other, maps, adapters, rank, planes, span):
    mp_count, _, lanes = maps.shape
    rows = ids.shape[0]
    depth = planes * span // lanes * adapters * rank
    return pl.pallas_call(
        functools.partial(delta_kernel, adapters, rank),
        in_specs=[WHOLE] * 3 + [ANYWHERE],
        out_specs=WHOLE,
        out_shape=jax.ShapeDtypeStruct((planes, rows, span), jnp.bfloat16),
        scratch_shapes=[pltpu.VMEM((mp_count, depth, lanes), maps.dtype), pltpu.SemaphoreType.DMA],
        compiler_params=params(),
        cost_estimate=cost(2 * rows * mp_count * depth * lanes, 2 * mp_count * depth * lanes),
    )(ids, mine, other, maps)


def finish_kernel(mp_count, turns, info_ref, delta_ref, *rest):
    parts, (delta, own, others, done, sems) = rest[: mp_count * turns], rest[-5:]
    out, *away = rest[-6 - turns : -5]
    rows, span = away[0].shape
    each = mp_count + 1
    loads = []
    for turn in range(turns):
        first, *peers = parts[mp_count * turn : mp_count * (turn + 1)]
        pairs = [(first, own.at[turn]), (delta_ref.at[info_ref[2 * turn]], delta.at[turn])]
        pairs += [(part, others.at[turn, n]) for n, part in enumerate(peers)]
        loads.append(start_all(pairs, sems.at[pl.ds(turn * each, each)]))
    stores = []
    for turn in range(turns):
        for load in loads[turn]:
            load.wait()
        total = own[turn]
        for n in range(mp_count - 1):
            total = total + others[turn, n].astype(jnp.float32)
        done[turn] = (total + delta[turn].astype(jnp.float32)).astype(done.dtype)
        place = pl.ds(pl.multiple_of(info_ref[2 * turn + 1] * span, span), span)
        pairs = [(done.at[turn, rows:, :], away[turn]), (done.at[turn, :rows, :], out.at[:, place])]
        stores += start_all(pairs, sems.at[pl.ds(turns * each + 2 * turn, 2)])
    for store in stores:
        store.wait()


def finish(info, delta, parts, held, width):
    turns, mp_count = len(parts), len(parts[0])
    rows, span = parts[0][0].shape
    operands = [info, delta, *sum(parts, [])] + ([] if held is None else [held])
    away = jax.ShapeDtypeStruct((rows // CORES, span), delta.dtype)
    return pl.pallas_call(
        functools.partial(finish_kernel, mp_count, turns),
        in_specs=[SCALARS] + [ANYWHERE] * (len(operands) - 1),
        out_specs=[ANYWHERE] * (1 + turns),
        out_shape=[jax.ShapeDtypeStruct((rows // CORES, width), delta.dtype)] + [away] * turns,
        scratch_shapes=[
            pltpu.VMEM((turns, rows, span), delta.dtype),
            pltpu.VMEM((turns, rows, span), jnp.float32),
            pltpu.VMEM((turns, mp_count - 1, rows, span), delta.dtype),
            pltpu.VMEM((turns, rows, span), delta.dtype),
            pltpu.SemaphoreType.DMA((turns * (mp_count + 3),)),
        ],
        input_output_aliases={} if held is None else {len(operands) - 1: 0},
        compiler_params=params(),
        cost_estimate=cost(4 * rows * span * turns, 12 * rows * span * turns),
    )(*operands)


def settle_kernel(info_ref, *rest):
    pieces, (out, sems) = rest[:-3], rest[-2:]
    span = pieces[0].shape[1]
    load_all(
        [
            (piece, out.at[:, pl.ds(pl.multiple_of(info_ref[n] * span, span), span)])
            for n, piece in enumerate(pieces)
        ],
        sems,
    )


def settle(info, pieces, held):
    operands = [info, *pieces, held]
    return pl.pallas_call(
        settle_kernel,
        in_specs=[SCALARS] + [WHOLE] * len(pieces) + [ANYWHERE],
        out_specs=ANYWHERE,
        out_shape=jax.ShapeDtypeStruct(held.shape, held.dtype),
        scratch_shapes=[pltpu.SemaphoreType.DMA((len(pieces),))],
        input_output_aliases={len(operands) - 1: 0},
        compiler_params=params(),
        cost_estimate=cost(0, 4 * len(pieces) * pieces[0].size),
    )(*operands)


def by_plane(plane, values):
    return sum(jnp.where(plane == n, value, 0) for n, value in enumerate(values)).astype(jnp.int32)


def arrival_order(plane, planes):
    sides = (1, -1) if 2 * plane < planes else (-1, 1)
    return [
        (side, distance)
        for distance in range(1, planes)
        for side in sides
        if 0 <= plane + side * distance < planes
    ]


def local(tokens, frozen_weight, adapter_down_weight, adapter_up_weight, token_adapter_index):
    mp_count, dp_count = lax.axis_size("mp"), lax.axis_size("dp")
    position, replica = lax.axis_index("mp"), lax.axis_index("dp")
    planes = dp_count // CORES
    plane, core = replica // CORES, replica % CORES
    group_rows, features = tokens.shape
    rows = group_rows // mp_count
    width = frozen_weight.shape[1]
    adapters, rank, up_span = adapter_up_weight.shape[1:]
    ranks = adapters * rank

    def info_of(*values):
        return jnp.stack([jnp.asarray(value, jnp.int32) for value in values])

    def after_all(*arrays):
        return lax.optimization_barrier(arrays)

    def swap(array):
        return lax.ppermute(array, "dp", [(n, n ^ 1) for n in range(dp_count)])

    def trade(array):
        return lax.all_to_all(array, "mp", 0, 0)

    def pass_round(blocks):
        return [
            lax.ppermute(block, "mp", [(m, m ^ n) for m in range(mp_count)]) for n, block in enumerate(blocks, 1)
        ]

    def hop(array, side, step):
        sources = range(1, planes - step + 1) if side > 0 else range(step - 1, planes - 1)
        return lax.ppermute(
            array, "dp", [(CORES * n + m, CORES * (n - side) + m) for n in sources for m in range(CORES)]
        )

    got = {(side, 1): hop(frozen_weight, side, 1) for side in (1, -1)}
    other = swap(tokens)
    ids = token_adapter_index.reshape(group_rows, 1)
    ids = jnp.stack([ids, swap(token_adapter_index).reshape(group_rows, 1)])
    own_ids = lax.dynamic_slice_in_dim(ids, position * rows, rows, axis=1).reshape(CORES * rows, 1)

    core_of = core.astype(jnp.int32).reshape(1)
    down = trade(cut_down(core_of, adapter_down_weight, mp_count))
    up = cut_up(core_of, adapter_up_weight.reshape(2, ranks, up_span), mp_count, width, down.shape[2])

    own, *sent = base_products(info_of(position, 0), tokens, other, [frozen_weight], mp_count, COVER, up, ids, own_ids)
    parts = [own] + pass_round(sent)
    finished = []
    group = plane
    orders = [arrival_order(n, planes) for n in range(planes)]
    for turn in range(1, planes):
        if turn < planes - 1:
            got[1, turn], got[-1, turn], parts[0] = after_all(got[1, turn], got[-1, turn], parts[0])
            for side in (1, -1):
                got[side, turn + 1] = hop(got[side, turn], side, turn + 1)
        wanted = [order[turn - 1] for order in orders]
        options = sorted(set(wanted))
        choice = by_plane(plane, [options.index(item) for item in wanted])
        before = []
        if turn == planes - 1:
            sums = trade(sums)
            before = [sums]
        elif turn == 1:
            before = [down]
        else:
            before = finished[turn - 2][1][1:]
        finished.append((group, parts))
        group = by_plane(plane, [n + side * distance for n, (side, distance) in enumerate(wanted)])
        info = info_of(position, choice)
        shards = [got[option] for option in options]
        last = turn == planes - 1
        own, *sent = base_products(info, tokens, other, shards, mp_count, COVER, *before)
        parts = [own] + pass_round(sent)
        if turn == 1:
            up, own = after_all(up, own)
            up = trade(up)
            parts[0] = own
        elif turn == 2 and not last:
            sums = low_sums(core_of, tokens, other, ids, down, adapters, rank, own, up, *finished[1][1][1:])
    finished.append((group, parts))

    delta = deltas_of(own_ids, sums, swap(sums), up, adapters, rank, planes, width)
    out, places, pieces = None, [], []
    for some in (finished[:-1], finished[-1:]):
        info = info_of(*[value for group, _ in some for value in (group, CORES * group + core)])
        out, *away = finish(info, delta, [parts for _, parts in some], out, dp_count * width)
        places.append(info_of(*[CORES * group + 1 - core for group, _ in some]))
        pieces.append([swap(piece) for piece in away])
    for place, some in zip(places, pieces):
        out = settle(place, some, out)
    return out


def solution(mesh):
    placed = (P("dp", "mp"), P("mp", "dp"), P(None, "mp"), P(None, "mp", None, None), P("dp"))
    return jax.shard_map(
        local, mesh=mesh, in_specs=placed, out_specs=P(("dp", "mp"), None), check_vma=False
    )
```

```python
import functools

import jax
import jax.numpy as jnp
from jax import lax
from jax.experimental import pallas as pl
from jax.experimental.pallas import tpu as pltpu
from jax.sharding import PartitionSpec as P

ADAPTER_SCALE = 2.0
CORES = 2
LANES = 128
COVER = 64
VMEM_BYTES = 60 * 1024 * 1024
ANYWHERE = pl.BlockSpec(memory_space=pl.ANY)
WHOLE = pl.BlockSpec(memory_space=pltpu.VMEM)
SCALARS = pl.BlockSpec(memory_space=pltpu.SMEM)


def params():
    return pltpu.CompilerParams(vmem_limit_bytes=VMEM_BYTES)


def cost(flops, bytes_accessed):
    return pl.CostEstimate(flops=flops, bytes_accessed=bytes_accessed, transcendentals=0)


def start_all(pairs, sems):
    copies = [pltpu.make_async_copy(src, dst, sems.at[n]) for n, (src, dst) in enumerate(pairs)]
    for copy in copies:
        copy.start()
    return copies


def load_all(pairs, sems):
    for copy in start_all(pairs, sems):
        copy.wait()


def base_kernel(mp_count, count, kept, at, info_ref, mine_ref, other_ref, *rest):
    choices = rest[:count]
    weight, done, own, sems = rest[-4:] if kept else [*rest[-5:-4], *rest[-3:]]
    outs = rest[-4 - mp_count : -4] if kept else rest[-5 - mp_count : -5]
    rows = own.shape[0] // CORES
    for number, choice in enumerate(choices):

        @pl.when(info_ref[at] == number)
        def _(choice=choice):
            pltpu.make_async_copy(choice, weight, sems.at[0]).start()

    order = [(number, part) for number in reversed(range(mp_count)) for part in range(CORES)]
    blocks, copies = {}, []
    for number, part in order:
        place = pl.ds(pl.multiple_of((info_ref[0] ^ number) * rows, rows), rows)
        source = (mine_ref, other_ref)[part].at[place, :]
        n = CORES * number + part
        blocks[n] = source if kept else rest[-4].at[n]
        if not kept:
            copies.append(pltpu.make_async_copy(source, blocks[n], sems.at[1 + n]))
            copies[-1].start()
    pltpu.make_async_copy(choices[0], weight, sems.at[0]).wait()
    stores = []
    for turn, (number, part) in enumerate(order):
        if not kept:
            copies[turn].wait()
        target = done.at[number] if number else own
        product = jnp.dot(blocks[CORES * number + part][...], weight[...], preferred_element_type=jnp.float32)
        target[part * rows : (part + 1) * rows, :] = product.astype(target.dtype)
        if part:
            stores.append(pltpu.make_async_copy(target, outs[number], sems.at[1 + CORES * mp_count + number]))
            stores[-1].start()
    for store in stores:
        store.wait()


def base_products(info, at, mine, other, choices, mp_count, kept, *before):
    group_rows, features = mine.shape
    rows, span = group_rows // mp_count, choices[0].shape[1]
    return pl.pallas_call(
        functools.partial(base_kernel, mp_count, len(choices), kept, at),
        in_specs=[SCALARS] + [WHOLE if kept else ANYWHERE] * 2 + [ANYWHERE] * (len(choices) + len(before)),
        out_specs=[ANYWHERE] * mp_count,
        scratch_shapes=[pltpu.VMEM((features, span), mine.dtype)]
        + ([] if kept else [pltpu.VMEM((CORES * mp_count, rows, features), mine.dtype)])
        + [
            pltpu.VMEM((mp_count, CORES * rows, span), jnp.bfloat16),
            pltpu.VMEM((CORES * rows, span), jnp.float32),
            pltpu.SemaphoreType.DMA((1 + (1 + CORES) * mp_count,)),
        ],
        out_shape=[
            jax.ShapeDtypeStruct((CORES * rows, span), jnp.bfloat16 if number else jnp.float32)
            for number in range(mp_count)
        ],
        compiler_params=pltpu.CompilerParams(vmem_limit_bytes=VMEM_BYTES // 4 if kept else VMEM_BYTES),
        cost_estimate=cost(
            COVER * 2 * CORES * group_rows * features * span,
            2 * (CORES * group_rows * (features + span) + features * span),
        ),
    )(info, mine, other, *choices, *before)


def cut_down_kernel(info_ref, down_ref, out, block, sems):
    mp_count, features, lanes = block.shape
    mine = pl.ds(pl.multiple_of(info_ref[1] * lanes, lanes), lanes)
    loads = start_all(
        [(down_ref.at[n * features : (n + 1) * features, mine], block.at[n]) for n in range(mp_count)], sems
    )
    stores = []
    for n, load in enumerate(loads):
        load.wait()
        stores.append(pltpu.make_async_copy(block.at[n], out.at[n], sems.at[mp_count + n]))
        stores[-1].start()
    for store in stores:
        store.wait()


def cut_down(info, down, mp_count):
    shape = mp_count, down.shape[0] // mp_count, down.shape[1] // CORES
    return pl.pallas_call(
        cut_down_kernel,
        in_specs=[SCALARS, ANYWHERE],
        out_specs=ANYWHERE,
        out_shape=jax.ShapeDtypeStruct(shape, down.dtype),
        scratch_shapes=[pltpu.VMEM(shape, down.dtype), pltpu.SemaphoreType.DMA((2 * mp_count,))],
        compiler_params=params(),
        cost_estimate=cost(0, 2 * down.size),
    )(info, down)


def cut_up_kernel(width, info_ref, up_ref, out, block, sems):
    parts, ranks, span = up_ref.shape
    lanes = block.shape[1]
    pairs = []
    for part in range(parts):
        for place in range(0, span, CORES * width):
            for first in range(place, place + width, lanes):
                columns = pl.ds(pl.multiple_of(first + info_ref[1] * width, lanes), lanes)
                row = len(pairs) * ranks
                pairs.append((up_ref.at[part, :, columns], block.at[row : row + ranks, :]))
    load_all(pairs, sems)
    load_all([(block, out.at[n]) for n in range(out.shape[0])], sems)


def cut_up(info, up, mp_count, width, lanes):
    parts, ranks, span = up.shape
    blocks = parts * span // CORES // lanes
    return pl.pallas_call(
        functools.partial(cut_up_kernel, width),
        in_specs=[SCALARS, ANYWHERE],
        out_specs=ANYWHERE,
        out_shape=jax.ShapeDtypeStruct((mp_count, blocks * ranks, lanes), up.dtype),
        scratch_shapes=[
            pltpu.VMEM((blocks * ranks, lanes), up.dtype),
            pltpu.SemaphoreType.DMA((max(blocks, mp_count),)),
        ],
        compiler_params=params(),
        cost_estimate=cost(0, 4 * mp_count * blocks * ranks * lanes),
    )(info, up)


def low_kernel(adapters, rank_pair, info_ref, mine_ref, other_ref, mine_ids, other_ids, maps_ref, out, maps, sems):
    mp_count, features, lanes = maps.shape
    rows = mine_ref.shape[0] // mp_count
    load_all([(maps_ref.at[number, :features, :], maps.at[number]) for number in range(mp_count)], sems)
    lane_adapter = lax.broadcasted_iota(jnp.int32, (rows, lanes), 1) // rank_pair
    groups = lanes // rank_pair
    depth = CORES * rows // groups
    lane_group = lax.broadcasted_iota(jnp.int32, (depth, lanes), 1) // rank_pair
    for number in range(mp_count):
        halves = []
        for part in range(CORES):
            place = slice(number * rows, (number + 1) * rows)
            ids = (mine_ids, other_ids)[part][place, :]
            values = (mine_ref, other_ref)[part][place, :]
            total = jnp.zeros((rows, lanes), jnp.float32)
            for owner in range(0, mp_count, CORES):
                both = jnp.concatenate([maps[owner], maps[owner + 1]], axis=1)
                product = jnp.dot(values, both, preferred_element_type=jnp.float32)
                for m in range(CORES):
                    wanted = ids - (owner + m) * adapters - info_ref[1] * groups
                    total += jnp.where(lane_adapter == wanted, product[:, m * lanes : (m + 1) * lanes], 0.0)
            shift = lanes // 2
            while shift >= rank_pair:
                total = total + pltpu.roll(total, shift, 1)
                shift //= 2
            halves.append(total)
        both = jnp.concatenate(halves, axis=0)
        packed = jnp.zeros((depth, lanes), jnp.float32)
        for group in range(groups):
            packed += jnp.where(lane_group == group, both[group * depth : (group + 1) * depth, :], 0.0)
        out[number] = packed


def low_sums(info, mine, other, ids, maps, adapters, rank):
    group_rows, features = mine.shape
    mp_count, _, lanes = maps.shape
    rows = group_rows // mp_count
    depth = CORES * rows * 2 * rank // lanes
    return pl.pallas_call(
        functools.partial(low_kernel, adapters, 2 * rank),
        in_specs=[SCALARS] + [WHOLE] * 4 + [ANYWHERE],
        out_specs=WHOLE,
        out_shape=jax.ShapeDtypeStruct((mp_count, depth, lanes), jnp.float32),
        scratch_shapes=[pltpu.VMEM((mp_count, features, lanes), maps.dtype), pltpu.SemaphoreType.DMA((mp_count,))],
        compiler_params=pltpu.CompilerParams(vmem_limit_bytes=VMEM_BYTES // 4),
        cost_estimate=cost(
            2 * CORES * group_rows * features * mp_count * lanes, 2 * features * (CORES * group_rows + mp_count * lanes)
        ),
    )(info, mine, other, *ids, maps)


def delta_kernel(adapters, rank, info_ref, mine_ids, other_ids, mine_ref, other_ref, maps_ref, out, maps, sem):
    copy = pltpu.make_async_copy(maps_ref.at[:, maps_ref.shape[1] - maps.shape[1] :, :], maps, sem)
    copy.start()
    mp_count = maps.shape[0]
    planes, rows, span = out.shape
    lanes = mine_ref.shape[2]
    rank_pair = 2 * rank
    groups = lanes // rank_pair
    depth = rows // groups
    packed = sum(mine_ref[n] for n in range(mp_count))
    packed = packed + pltpu.roll(sum(other_ref[n] for n in range(mp_count)), lanes // 2, 1)
    lane_group = lax.broadcasted_iota(jnp.int32, (depth, lanes), 1) // rank_pair
    spread = []
    for group in range(groups):
        values = jnp.where(lane_group == group, packed, 0.0)
        shift = lanes // 2
        while shift >= rank_pair:
            values = values + pltpu.roll(values, shift, 1)
            shift //= 2
        spread.append(values)
    low = jnp.concatenate(spread, axis=0)
    place = pl.ds(pl.multiple_of(info_ref[0] * (rows // CORES), rows // CORES), rows // CORES)
    ids = jnp.concatenate([mine_ids[place, :], other_ids[place, :]], axis=0)
    lane_block = lax.broadcasted_iota(jnp.int32, (rows, lanes), 1) // rank
    even = lane_block % 2 == 0
    lows = [jnp.where(even, low, pltpu.roll(low, rank, 1)), jnp.where(even, pltpu.roll(low, lanes - rank, 1), low)]
    copy.wait()
    ranks = adapters * rank
    for part in range(2):
        spreads = [
            jnp.where(lane_block == ids - owner * adapters, lows[part], 0.0).astype(jnp.bfloat16)
            for owner in range(mp_count)
        ]
        for plane in range(part * planes // 2, (part + 1) * planes // 2):
            for piece in range(span // lanes):
                first = (plane * (span // lanes) + piece) * ranks
                total = jnp.zeros((rows, lanes), jnp.float32)
                for owner in range(mp_count):
                    weights = maps[owner, first : first + ranks, :]
                    total += jnp.dot(spreads[owner], weights, preferred_element_type=jnp.float32)
                out[plane, :, piece * lanes : (piece + 1) * lanes] = (ADAPTER_SCALE * total).astype(out.dtype)


def deltas_of(info, ids, mine, other, maps, adapters, rank, planes, span):
    mp_count, _, lanes = maps.shape
    rows = CORES * ids[0].shape[0] // mp_count
    depth = planes * span // lanes * adapters * rank
    return pl.pallas_call(
        functools.partial(delta_kernel, adapters, rank),
        in_specs=[SCALARS] + [WHOLE] * 4 + [ANYWHERE],
        out_specs=WHOLE,
        out_shape=jax.ShapeDtypeStruct((planes, rows, span), jnp.bfloat16),
        scratch_shapes=[pltpu.VMEM((mp_count, depth, lanes), maps.dtype), pltpu.SemaphoreType.DMA],
        compiler_params=params(),
        cost_estimate=cost(2 * rows * mp_count * depth * lanes, 2 * mp_count * depth * lanes),
    )(info, *ids, mine, other, maps)


def finish_kernel(mp_count, places, info_ref, delta_ref, *rest):
    turns = len(places)
    parts, (delta, own, others, done, sems) = rest[: mp_count * turns], rest[-5:]
    out, *away = rest[-6 - turns : -5]
    rows, span = away[0].shape
    each = mp_count + 1
    loads = []
    for turn in range(turns):
        first, *peers = parts[mp_count * turn : mp_count * (turn + 1)]
        pairs = [(first, own.at[turn]), (delta_ref.at[info_ref[places[turn]]], delta.at[turn])]
        pairs += [(part, others.at[turn, n]) for n, part in enumerate(peers)]
        loads.append(start_all(pairs, sems.at[pl.ds(turn * each, each)]))
    stores = []
    for turn in range(turns):
        for load in loads[turn]:
            load.wait()
        total = own[turn]
        for n in range(mp_count - 1):
            total = total + others[turn, n].astype(jnp.float32)
        done[turn] = (total + delta[turn].astype(jnp.float32)).astype(done.dtype)
        place = pl.ds(pl.multiple_of(info_ref[places[turn] + 1] * span, span), span)
        pairs = [(done.at[turn, rows:, :], away[turn]), (done.at[turn, :rows, :], out.at[:, place])]
        stores += start_all(pairs, sems.at[pl.ds(turns * each + 2 * turn, 2)])
    for store in stores:
        store.wait()


def finish(info, places, delta, parts, held, width):
    turns, mp_count = len(parts), len(parts[0])
    rows, span = parts[0][0].shape
    operands = [info, delta, *sum(parts, [])] + ([] if held is None else [held])
    away = jax.ShapeDtypeStruct((rows // CORES, span), delta.dtype)
    return pl.pallas_call(
        functools.partial(finish_kernel, mp_count, places),
        in_specs=[SCALARS] + [ANYWHERE] * (len(operands) - 1),
        out_specs=[ANYWHERE] * (1 + turns),
        out_shape=[jax.ShapeDtypeStruct((rows // CORES, width), delta.dtype)] + [away] * turns,
        scratch_shapes=[
            pltpu.VMEM((turns, rows, span), delta.dtype),
            pltpu.VMEM((turns, rows, span), jnp.float32),
            pltpu.VMEM((turns, mp_count - 1, rows, span), delta.dtype),
            pltpu.VMEM((turns, rows, span), delta.dtype),
            pltpu.SemaphoreType.DMA((turns * (mp_count + 3),)),
        ],
        input_output_aliases={} if held is None else {len(operands) - 1: 0},
        compiler_params=params(),
        cost_estimate=cost(4 * rows * span * turns, 12 * rows * span * turns),
    )(*operands)


def settle_kernel(places, info_ref, *rest):
    pieces, (out, sems) = rest[:-3], rest[-2:]
    span = pieces[0].shape[1]
    load_all(
        [
            (piece, out.at[:, pl.ds(pl.multiple_of(info_ref[places[n]] * span, span), span)])
            for n, piece in enumerate(pieces)
        ],
        sems,
    )


def settle(info, places, pieces, held):
    operands = [info, *pieces, held]
    return pl.pallas_call(
        functools.partial(settle_kernel, places),
        in_specs=[SCALARS] + [WHOLE] * len(pieces) + [ANYWHERE],
        out_specs=ANYWHERE,
        out_shape=jax.ShapeDtypeStruct(held.shape, held.dtype),
        scratch_shapes=[pltpu.SemaphoreType.DMA((len(pieces),))],
        input_output_aliases={len(operands) - 1: 0},
        compiler_params=params(),
        cost_estimate=cost(0, 4 * len(pieces) * pieces[0].size),
    )(*operands)


def by_plane(plane, values):
    return sum(jnp.where(plane == n, value, 0) for n, value in enumerate(values)).astype(jnp.int32)


def arrival_order(plane, planes):
    sides = (1, -1) if 2 * plane < planes else (-1, 1)
    return [
        (side, distance)
        for distance in range(1, planes)
        for side in sides
        if 0 <= plane + side * distance < planes
    ]


def local(tokens, frozen_weight, adapter_down_weight, adapter_up_weight, token_adapter_index):
    mp_count, dp_count = lax.axis_size("mp"), lax.axis_size("dp")
    position, replica = lax.axis_index("mp"), lax.axis_index("dp")
    planes = dp_count // CORES
    plane, core = replica // CORES, replica % CORES
    group_rows, features = tokens.shape
    rows = group_rows // mp_count
    width = frozen_weight.shape[1]
    adapters, rank, up_span = adapter_up_weight.shape[1:]
    ranks = adapters * rank

    def after_all(*arrays):
        return lax.optimization_barrier(arrays)

    def swap(array):
        return lax.ppermute(array, "dp", [(n, n ^ 1) for n in range(dp_count)])

    def trade(array):
        return lax.all_to_all(array, "mp", 0, 0)

    def pass_round(blocks):
        return [
            lax.ppermute(block, "mp", [(m, m ^ n) for m in range(mp_count)]) for n, block in enumerate(blocks, 1)
        ]

    def hop(array, side, step):
        sources = range(1, planes - step + 1) if side > 0 else range(step - 1, planes - 1)
        return lax.ppermute(
            array, "dp", [(CORES * n + m, CORES * (n - side) + m) for n in sources for m in range(CORES)]
        )

    got = {(side, 1): hop(frozen_weight, side, 1) for side in (1, -1)}
    other = swap(tokens)
    ids = token_adapter_index.reshape(group_rows, 1)
    ids = [ids, swap(token_adapter_index).reshape(group_rows, 1)]

    orders = [[(0, 0)] + arrival_order(n, planes) for n in range(planes)]
    options = [sorted({order[turn] for order in orders}) for turn in range(planes)]
    scalars = [position, core]
    choice_at, group_at = [], []
    for turn in range(planes):
        wanted = [order[turn] for order in orders]
        choice_at.append(len(scalars))
        scalars.append(by_plane(plane, [options[turn].index(item) for item in wanted]))
        group = by_plane(plane, [n + side * distance for n, (side, distance) in enumerate(wanted)])
        group_at.append(len(scalars))
        scalars += [group, CORES * group + core, CORES * group + 1 - core]
    info = jnp.stack([jnp.asarray(value, jnp.int32) for value in scalars])

    down = trade(cut_down(info, adapter_down_weight, mp_count))
    up = cut_up(info, adapter_up_weight.reshape(2, ranks, up_span), mp_count, width, down.shape[2])
    own, *sent = base_products(info, choice_at[0], tokens, other, [frozen_weight], mp_count, False, up, *ids)
    finished, out, away = [], None, []

    def finish_some(turns, out):
        places = [group_at[turn] for turn in turns]
        return finish(info, places, delta, [finished[turn] for turn in turns], out, dp_count * width)

    for turn in range(1, planes):
        last = turn == planes - 1
        if not last:
            got[1, turn], got[-1, turn], own = after_all(got[1, turn], got[-1, turn], own)
            for side in (1, -1):
                got[side, turn + 1] = hop(got[side, turn], side, turn + 1)
        finished.append([own] + pass_round(sent))
        before = []
        if turn == 1:
            sums = low_sums(info, tokens, other, ids, down, adapters, rank)
            before = [sums, *finished[0][1:]]
        elif turn == 2:
            up = trade(up)
            before = [up]
        if last:
            sums, finished[-1][0], *finished[-2][1:] = after_all(sums, own, *finished[-2][1:])
            sums = trade(sums)
            delta = deltas_of(info, ids, sums, swap(sums), up, adapters, rank, planes, width)
            before = [delta]
        shards = [got[option] for option in options[turn]]
        kept = turn == 1 or last
        own, *sent = base_products(info, choice_at[turn], tokens, other, shards, mp_count, kept, *before)
    finished.append([own] + pass_round(sent))

    for turns in (range(planes - 2), [planes - 2], [planes - 1]):
        out, *pieces = finish_some(turns, out)
        away += pieces
    away = [swap(piece) for piece in away]
    places = [at + 2 for at in group_at]
    out = settle(info, places[:-1], away[:-1], out)
    return settle(info, places[-1:], away[-1:], out)


def solution(mesh):
    placed = (P("dp", "mp"), P("mp", "dp"), P(None, "mp"), P(None, "mp", None, None), P("dp"))
    return jax.shard_map(
        local, mesh=mesh, in_specs=placed, out_specs=P(("dp", "mp"), None), check_vma=False
    )
```

```python
import functools

import jax
import jax.numpy as jnp
from jax import lax
from jax.experimental import pallas as pl
from jax.experimental.pallas import tpu as pltpu
from jax.sharding import PartitionSpec as P

ADAPTER_SCALE = 2.0
CORES = 2
LANES = 128
COVER = 64
VMEM_BYTES = 60 * 1024 * 1024
ANYWHERE = pl.BlockSpec(memory_space=pl.ANY)
WHOLE = pl.BlockSpec(memory_space=pltpu.VMEM)
SCALARS = pl.BlockSpec(memory_space=pltpu.SMEM)


def params():
    return pltpu.CompilerParams(vmem_limit_bytes=VMEM_BYTES)


def cost(flops, bytes_accessed):
    return pl.CostEstimate(flops=flops, bytes_accessed=bytes_accessed, transcendentals=0)


def start_all(pairs, sems):
    copies = [pltpu.make_async_copy(src, dst, sems.at[n]) for n, (src, dst) in enumerate(pairs)]
    for copy in copies:
        copy.start()
    return copies


def load_all(pairs, sems):
    for copy in start_all(pairs, sems):
        copy.wait()


def base_kernel(mp_count, counts, kept, places, info_ref, mine_ref, other_ref, *rest):
    total = sum(counts)
    choices = rest[:total]
    weight, done, own, sems = rest[-4:] if kept else [*rest[-5:-4], *rest[-3:]]
    outs = rest[-4 - mp_count : -4] if kept else rest[-5 - mp_count : -5]
    rows = own.shape[0] // CORES
    span = weight.shape[2]
    first = 0
    for group, count in enumerate(counts):
        for number in range(count):

            @pl.when(info_ref[places[group]] == number)
            def _(group=group, choice=choices[first + number]):
                pltpu.make_async_copy(choice, weight.at[group], sems.at[group]).start()

        first += count

    order = [(number, part) for number in reversed(range(mp_count)) for part in range(CORES)]
    blocks, copies = {}, []
    for number, part in order:
        place = pl.ds(pl.multiple_of((info_ref[0] ^ number) * rows, rows), rows)
        source = (mine_ref, other_ref)[part].at[place, :]
        n = CORES * number + part
        blocks[n] = source if kept else rest[-4].at[n]
        if not kept:
            copies.append(pltpu.make_async_copy(source, blocks[n], sems.at[len(counts) + n]))
            copies[-1].start()
    for group in range(len(counts)):
        pltpu.make_async_copy(choices[0], weight.at[group], sems.at[group]).wait()
    stores = []
    for turn, (number, part) in enumerate(order):
        if not kept:
            copies[turn].wait()
        target = done.at[number] if number else own
        for group in range(len(counts)):
            product = jnp.dot(
                blocks[CORES * number + part][...], weight[group], preferred_element_type=jnp.float32
            )
            columns = slice(group * span, (group + 1) * span)
            target[part * rows : (part + 1) * rows, columns] = product.astype(target.dtype)
        if part:
            sem = sems.at[len(counts) + CORES * mp_count + number]
            stores.append(pltpu.make_async_copy(target, outs[number], sem))
            stores[-1].start()
    for store in stores:
        store.wait()


def base_products(info, places, mine, other, groups, mp_count, kept, cover, *before):
    group_rows, features = mine.shape
    rows, span = group_rows // mp_count, groups[0][0].shape[1]
    wide = span * len(groups)
    shards = [shard for group in groups for shard in group]
    return pl.pallas_call(
        functools.partial(base_kernel, mp_count, [len(group) for group in groups], kept, places),
        in_specs=[SCALARS] + [WHOLE if kept else ANYWHERE] * 2 + [ANYWHERE] * (len(shards) + len(before)),
        out_specs=[ANYWHERE] * mp_count,
        scratch_shapes=[pltpu.VMEM((len(groups), features, span), mine.dtype)]
        + ([] if kept else [pltpu.VMEM((CORES * mp_count, rows, features), mine.dtype)])
        + [
            pltpu.VMEM((mp_count, CORES * rows, wide), jnp.bfloat16),
            pltpu.VMEM((CORES * rows, wide), jnp.float32),
            pltpu.SemaphoreType.DMA((len(groups) + (1 + CORES) * mp_count,)),
        ],
        out_shape=[
            jax.ShapeDtypeStruct((CORES * rows, wide), jnp.bfloat16 if number else jnp.float32)
            for number in range(mp_count)
        ],
        compiler_params=pltpu.CompilerParams(vmem_limit_bytes=VMEM_BYTES // 4 if kept else VMEM_BYTES),
        cost_estimate=cost(
            cover * 2 * CORES * group_rows * features * wide,
            2 * (CORES * group_rows * (features + wide) + features * wide),
        ),
    )(info, mine, other, *shards, *before)


def cut_down_kernel(info_ref, down_ref, out, block, sems):
    mp_count, features, lanes = block.shape
    mine = pl.ds(pl.multiple_of(info_ref[1] * lanes, lanes), lanes)
    loads = start_all(
        [(down_ref.at[n * features : (n + 1) * features, mine], block.at[n]) for n in range(mp_count)], sems
    )
    stores = []
    for n, load in enumerate(loads):
        load.wait()
        stores.append(pltpu.make_async_copy(block.at[n], out.at[n], sems.at[mp_count + n]))
        stores[-1].start()
    for store in stores:
        store.wait()


def cut_down(info, down, mp_count):
    shape = mp_count, down.shape[0] // mp_count, down.shape[1] // CORES
    return pl.pallas_call(
        cut_down_kernel,
        in_specs=[SCALARS, ANYWHERE],
        out_specs=ANYWHERE,
        out_shape=jax.ShapeDtypeStruct(shape, down.dtype),
        scratch_shapes=[pltpu.VMEM(shape, down.dtype), pltpu.SemaphoreType.DMA((2 * mp_count,))],
        compiler_params=params(),
        cost_estimate=cost(0, 2 * down.size),
    )(info, down)


def cut_up_kernel(width, info_ref, up_ref, out, block, sems):
    parts, ranks, span = up_ref.shape
    lanes = block.shape[1]
    pairs = []
    for part in range(parts):
        for place in range(0, span, CORES * width):
            for first in range(place, place + width, lanes):
                columns = pl.ds(pl.multiple_of(first + info_ref[1] * width, lanes), lanes)
                row = len(pairs) * ranks
                pairs.append((up_ref.at[part, :, columns], block.at[row : row + ranks, :]))
    load_all(pairs, sems)
    load_all([(block, out.at[n]) for n in range(out.shape[0])], sems)


def cut_up(info, up, mp_count, width, lanes):
    parts, ranks, span = up.shape
    blocks = parts * span // CORES // lanes
    return pl.pallas_call(
        functools.partial(cut_up_kernel, width),
        in_specs=[SCALARS, ANYWHERE],
        out_specs=ANYWHERE,
        out_shape=jax.ShapeDtypeStruct((mp_count, blocks * ranks, lanes), up.dtype),
        scratch_shapes=[
            pltpu.VMEM((blocks * ranks, lanes), up.dtype),
            pltpu.SemaphoreType.DMA((max(blocks, mp_count),)),
        ],
        compiler_params=params(),
        cost_estimate=cost(COVER * 2**32, 4 * mp_count * blocks * ranks * lanes),
    )(info, up)


def low_kernel(adapters, rank_pair, info_ref, mine_ref, other_ref, mine_ids, other_ids, maps_ref, _, out, maps, sems):
    mp_count, features, lanes = maps.shape
    rows = mine_ref.shape[0] // mp_count
    load_all([(maps_ref.at[number, :features, :], maps.at[number]) for number in range(mp_count)], sems)
    lane_adapter = lax.broadcasted_iota(jnp.int32, (rows, lanes), 1) // rank_pair
    groups = lanes // rank_pair
    depth = CORES * rows // groups
    lane_group = lax.broadcasted_iota(jnp.int32, (depth, lanes), 1) // rank_pair
    for number in range(mp_count):
        halves = []
        for part in range(CORES):
            place = slice(number * rows, (number + 1) * rows)
            ids = (mine_ids, other_ids)[part][place, :]
            values = (mine_ref, other_ref)[part][place, :]
            total = jnp.zeros((rows, lanes), jnp.float32)
            for owner in range(0, mp_count, CORES):
                both = jnp.concatenate([maps[owner], maps[owner + 1]], axis=1)
                product = jnp.dot(values, both, preferred_element_type=jnp.float32)
                for m in range(CORES):
                    wanted = ids - (owner + m) * adapters - info_ref[1] * groups
                    total += jnp.where(lane_adapter == wanted, product[:, m * lanes : (m + 1) * lanes], 0.0)
            shift = lanes // 2
            while shift >= rank_pair:
                total = total + pltpu.roll(total, shift, 1)
                shift //= 2
            halves.append(total)
        both = jnp.concatenate(halves, axis=0)
        packed = jnp.zeros((depth, lanes), jnp.float32)
        for group in range(groups):
            packed += jnp.where(lane_group == group, both[group * depth : (group + 1) * depth, :], 0.0)
        out[number] = packed


def low_sums(info, mine, other, ids, maps, adapters, rank, before):
    group_rows, features = mine.shape
    mp_count, _, lanes = maps.shape
    rows = group_rows // mp_count
    depth = CORES * rows * 2 * rank // lanes
    return pl.pallas_call(
        functools.partial(low_kernel, adapters, 2 * rank),
        in_specs=[SCALARS] + [WHOLE] * 4 + [ANYWHERE] * 2,
        out_specs=WHOLE,
        out_shape=jax.ShapeDtypeStruct((mp_count, depth, lanes), jnp.float32),
        scratch_shapes=[pltpu.VMEM((mp_count, features, lanes), maps.dtype), pltpu.SemaphoreType.DMA((mp_count,))],
        compiler_params=pltpu.CompilerParams(vmem_limit_bytes=VMEM_BYTES // 4),
        cost_estimate=cost(
            COVER * 2 * CORES * group_rows * features * mp_count * lanes,
            2 * features * (CORES * group_rows + mp_count * lanes)
        ),
    )(info, mine, other, *ids, maps, before)


def delta_kernel(adapters, rank, info_ref, mine_ids, other_ids, mine_ref, other_ref, maps_ref, out, maps, sem):
    copy = pltpu.make_async_copy(maps_ref.at[:, maps_ref.shape[1] - maps.shape[1] :, :], maps, sem)
    copy.start()
    mp_count = maps.shape[0]
    planes, rows, span = out.shape
    lanes = mine_ref.shape[2]
    rank_pair = 2 * rank
    groups = lanes // rank_pair
    depth = rows // groups
    packed = sum(mine_ref[n] for n in range(mp_count))
    packed = packed + pltpu.roll(sum(other_ref[n] for n in range(mp_count)), lanes // 2, 1)
    lane_group = lax.broadcasted_iota(jnp.int32, (depth, lanes), 1) // rank_pair
    spread = []
    for group in range(groups):
        values = jnp.where(lane_group == group, packed, 0.0)
        shift = lanes // 2
        while shift >= rank_pair:
            values = values + pltpu.roll(values, shift, 1)
            shift //= 2
        spread.append(values)
    low = jnp.concatenate(spread, axis=0)
    place = pl.ds(pl.multiple_of(info_ref[0] * (rows // CORES), rows // CORES), rows // CORES)
    ids = jnp.concatenate([mine_ids[place, :], other_ids[place, :]], axis=0)
    lane_block = lax.broadcasted_iota(jnp.int32, (rows, lanes), 1) // rank
    even = lane_block % 2 == 0
    lows = [jnp.where(even, low, pltpu.roll(low, rank, 1)), jnp.where(even, pltpu.roll(low, lanes - rank, 1), low)]
    copy.wait()
    ranks = adapters * rank
    for part in range(2):
        spreads = [
            jnp.where(lane_block == ids - owner * adapters, lows[part], 0.0).astype(jnp.bfloat16)
            for owner in range(mp_count)
        ]
        for plane in range(part * planes // 2, (part + 1) * planes // 2):
            for piece in range(span // lanes):
                first = (plane * (span // lanes) + piece) * ranks
                total = jnp.zeros((rows, lanes), jnp.float32)
                for owner in range(mp_count):
                    weights = maps[owner, first : first + ranks, :]
                    total += jnp.dot(spreads[owner], weights, preferred_element_type=jnp.float32)
                out[plane, :, piece * lanes : (piece + 1) * lanes] = (ADAPTER_SCALE * total).astype(out.dtype)


def deltas_of(info, ids, mine, other, maps, adapters, rank, planes, span):
    mp_count, _, lanes = maps.shape
    rows = CORES * ids[0].shape[0] // mp_count
    depth = planes * span // lanes * adapters * rank
    return pl.pallas_call(
        functools.partial(delta_kernel, adapters, rank),
        in_specs=[SCALARS] + [WHOLE] * 4 + [ANYWHERE],
        out_specs=WHOLE,
        out_shape=jax.ShapeDtypeStruct((planes, rows, span), jnp.bfloat16),
        scratch_shapes=[pltpu.VMEM((mp_count, depth, lanes), maps.dtype), pltpu.SemaphoreType.DMA],
        compiler_params=params(),
        cost_estimate=cost(2 * rows * mp_count * depth * lanes, 2 * mp_count * depth * lanes),
    )(info, *ids, mine, other, maps)


def finish_kernel(mp_count, places, info_ref, delta_ref, *rest):
    parts, (out, away, delta, own, others, done, sems) = rest[:mp_count], rest[-7:]
    groups, rows, span = delta.shape
    rows //= CORES
    pairs = [(parts[0], own)] + [(part, others.at[n]) for n, part in enumerate(parts[1:])]
    pairs += [(delta_ref.at[info_ref[place]], delta.at[group]) for group, place in enumerate(places)]
    load_all(pairs, sems)
    pairs = [(done.at[rows:, :], away)]
    for group, place in enumerate(places):
        columns = slice(group * span, (group + 1) * span)
        total = own[:, columns]
        for n in range(mp_count - 1):
            total = total + others[n, :, columns].astype(jnp.float32)
        done[:, columns] = (total + delta[group].astype(jnp.float32)).astype(done.dtype)
        target = pl.ds(pl.multiple_of(info_ref[place + 1] * span, span), span)
        pairs.append((done.at[:rows, columns], out.at[:, target]))
    load_all(pairs, sems)


def finish(info, places, delta, parts, held, width):
    mp_count, groups = len(parts), len(places)
    rows, wide = parts[0].shape
    operands = [info, delta, *parts] + ([] if held is None else [held])
    return pl.pallas_call(
        functools.partial(finish_kernel, mp_count, places),
        in_specs=[SCALARS] + [ANYWHERE] * (len(operands) - 1),
        out_specs=[ANYWHERE] * 2,
        out_shape=[
            jax.ShapeDtypeStruct((rows // CORES, width), delta.dtype),
            jax.ShapeDtypeStruct((rows // CORES, wide), delta.dtype),
        ],
        scratch_shapes=[
            pltpu.VMEM((groups, rows, wide // groups), delta.dtype),
            pltpu.VMEM((rows, wide), jnp.float32),
            pltpu.VMEM((mp_count - 1, rows, wide), delta.dtype),
            pltpu.VMEM((rows, wide), delta.dtype),
            pltpu.SemaphoreType.DMA((mp_count + groups,)),
        ],
        input_output_aliases={} if held is None else {len(operands) - 1: 0},
        compiler_params=params(),
        cost_estimate=cost(4 * rows * wide, 12 * rows * wide),
    )(*operands)


def settle_kernel(places, span, info_ref, *rest):
    pieces, (out, sems) = rest[: len(places)], rest[-2:]
    pairs = []
    for piece, some in zip(pieces, places):
        for group, place in enumerate(some):
            target = pl.ds(pl.multiple_of(info_ref[place] * span, span), span)
            pairs.append((piece.at[:, group * span : (group + 1) * span], out.at[:, target]))
    load_all(pairs, sems)


def settle(info, places, span, pieces, held):
    operands = [info, *pieces, held]
    return pl.pallas_call(
        functools.partial(settle_kernel, places, span),
        in_specs=[SCALARS] + [WHOLE] * len(pieces) + [ANYWHERE],
        out_specs=ANYWHERE,
        out_shape=jax.ShapeDtypeStruct(held.shape, held.dtype),
        scratch_shapes=[pltpu.SemaphoreType.DMA((sum(len(some) for some in places),))],
        input_output_aliases={len(operands) - 1: 0},
        compiler_params=params(),
        cost_estimate=cost(0, 4 * sum(piece.size for piece in pieces)),
    )(*operands)


def by_plane(plane, values):
    return sum(jnp.where(plane == n, value, 0) for n, value in enumerate(values)).astype(jnp.int32)


def arrival_order(plane, planes):
    sides = (1, -1) if 2 * plane < planes else (-1, 1)
    return [
        (side, distance)
        for distance in range(1, planes)
        for side in sides
        if 0 <= plane + side * distance < planes
    ]


def local(tokens, frozen_weight, adapter_down_weight, adapter_up_weight, token_adapter_index):
    mp_count, dp_count = lax.axis_size("mp"), lax.axis_size("dp")
    position, replica = lax.axis_index("mp"), lax.axis_index("dp")
    planes = dp_count // CORES
    plane, core = replica // CORES, replica % CORES
    group_rows, features = tokens.shape
    rows = group_rows // mp_count
    width = frozen_weight.shape[1]
    adapters, rank, up_span = adapter_up_weight.shape[1:]
    ranks = adapters * rank

    def after_all(*arrays):
        return lax.optimization_barrier(arrays)

    def swap(array):
        return lax.ppermute(array, "dp", [(n, n ^ 1) for n in range(dp_count)])

    def trade(array):
        return lax.all_to_all(array, "mp", 0, 0)

    def pass_round(blocks):
        return [
            lax.ppermute(block, "mp", [(m, m ^ n) for m in range(mp_count)]) for n, block in enumerate(blocks, 1)
        ]

    def hop(array, side, step):
        sources = range(1, planes - step + 1) if side > 0 else range(step - 1, planes - 1)
        return lax.ppermute(
            array, "dp", [(CORES * n + m, CORES * (n - side) + m) for n in sources for m in range(CORES)]
        )

    got = {(side, 1): hop(frozen_weight, side, 1) for side in (1, -1)}
    other = swap(tokens)
    ids = token_adapter_index.reshape(group_rows, 1)
    ids = [ids, swap(token_adapter_index).reshape(group_rows, 1)]

    orders = [[(0, 0)] + arrival_order(n, planes) for n in range(planes)]
    options = [sorted({order[turn] for order in orders}) for turn in range(planes)]
    scalars = [position, core]
    choice_at, group_at = [], []
    for turn in range(planes):
        wanted = [order[turn] for order in orders]
        choice_at.append(len(scalars))
        scalars.append(by_plane(plane, [options[turn].index(item) for item in wanted]))
        group = by_plane(plane, [n + side * distance for n, (side, distance) in enumerate(wanted)])
        group_at.append(len(scalars))
        scalars += [group, CORES * group + core, CORES * group + 1 - core]
    info = jnp.stack([jnp.asarray(value, jnp.int32) for value in scalars])

    down = trade(cut_down(info, adapter_down_weight, mp_count))
    up = cut_up(info, adapter_up_weight.reshape(2, ranks, up_span), mp_count, width, down.shape[2])
    got[1, 1], got[-1, 1], up = after_all(got[1, 1], got[-1, 1], up)
    finished, places = [], []

    for turn in range(1, planes):
        last = turn == planes - 1
        if not last:
            if turn > 1:
                got[1, turn], got[-1, turn], own, sums = after_all(got[1, turn], got[-1, turn], own, sums)
            for side in (1, -1):
                got[side, turn + 1] = hop(got[side, turn], side, turn + 1)
        if turn > 1:
            finished.append([own] + pass_round(sent))
        before = []
        if last:
            delta = deltas_of(info, ids, sums, swap(sums), up, adapters, rank, planes, width)
            before = [delta]
        elif turn == 2:
            sums = trade(sums)
            up, sums = after_all(up, sums)
            up = trade(up)
            before = finished[0][1:]
        turns = [0, 1] if turn == 1 else [turn]
        groups = [[frozen_weight] if n == 0 else [got[option] for option in options[n]] for n in turns]
        kept = turn == 1 or last
        cover = 1 if turn == 1 else COVER
        own, *sent = base_products(
            info, [choice_at[n] for n in turns], tokens, other, groups, mp_count, kept, cover, *before
        )
        places.append([group_at[n] for n in turns])
        if turn == 1:
            sums = low_sums(info, tokens, other, ids, down, adapters, rank, own)
    finished.append([own] + pass_round(sent))

    out, away = None, []
    for some, parts in zip(places, finished):
        out, piece = finish(info, some, delta, parts, out, dp_count * width)
        away.append(swap(piece))
    places = [[place + 2 for place in some] for some in places]
    out = settle(info, places[:-1], width, away[:-1], out)
    return settle(info, places[-1:], width, away[-1:], out)


def solution(mesh):
    placed = (P("dp", "mp"), P("mp", "dp"), P(None, "mp"), P(None, "mp", None, None), P("dp"))
    return jax.shard_map(
        local, mesh=mesh, in_specs=placed, out_specs=P(("dp", "mp"), None), check_vma=False
    )
```

```python
import functools

import jax
import jax.numpy as jnp
from jax import lax
from jax.experimental import pallas as pl
from jax.experimental.pallas import tpu as pltpu
from jax.sharding import PartitionSpec as P

ADAPTER_SCALE = 2.0
CORES = 2
LANES = 128
COVER = 64
VMEM_BYTES = 60 * 1024 * 1024
ANYWHERE = pl.BlockSpec(memory_space=pl.ANY)
WHOLE = pl.BlockSpec(memory_space=pltpu.VMEM)
SCALARS = pl.BlockSpec(memory_space=pltpu.SMEM)


def params():
    return pltpu.CompilerParams(vmem_limit_bytes=VMEM_BYTES)


def cost(flops, bytes_accessed):
    return pl.CostEstimate(flops=flops, bytes_accessed=bytes_accessed, transcendentals=0)


def start_all(pairs, sems):
    copies = [pltpu.make_async_copy(src, dst, sems.at[n]) for n, (src, dst) in enumerate(pairs)]
    for copy in copies:
        copy.start()
    return copies


def load_all(pairs, sems):
    for copy in start_all(pairs, sems):
        copy.wait()


def base_kernel(mp_count, counts, kept, places, info_ref, mine_ref, other_ref, *rest):
    total = sum(counts)
    choices = rest[:total]
    weight, done, own, sems = rest[-4:] if kept else [*rest[-5:-4], *rest[-3:]]
    outs = rest[-4 - mp_count : -4] if kept else rest[-5 - mp_count : -5]
    rows = own.shape[0] // CORES
    span = weight.shape[2]
    first = 0
    for group, count in enumerate(counts):
        for number in range(count):

            @pl.when(info_ref[places[group]] == number)
            def _(group=group, choice=choices[first + number]):
                pltpu.make_async_copy(choice, weight.at[group], sems.at[group]).start()

        first += count

    order = [(number, part) for number in reversed(range(mp_count)) for part in range(CORES)]
    blocks, copies = {}, []
    for number, part in order:
        place = pl.ds(pl.multiple_of((info_ref[0] ^ number) * rows, rows), rows)
        source = (mine_ref, other_ref)[part].at[place, :]
        n = CORES * number + part
        blocks[n] = source if kept else rest[-4].at[n]
        if not kept:
            copies.append(pltpu.make_async_copy(source, blocks[n], sems.at[len(counts) + n]))
            copies[-1].start()
    for group in range(len(counts)):
        pltpu.make_async_copy(choices[0], weight.at[group], sems.at[group]).wait()
    stores = []
    for turn, (number, part) in enumerate(order):
        if not kept:
            copies[turn].wait()
        target = done.at[number] if number else own
        for group in range(len(counts)):
            product = jnp.dot(
                blocks[CORES * number + part][...], weight[group], preferred_element_type=jnp.float32
            )
            columns = slice(group * span, (group + 1) * span)
            target[part * rows : (part + 1) * rows, columns] = product.astype(target.dtype)
        if part:
            sem = sems.at[len(counts) + CORES * mp_count + number]
            stores.append(pltpu.make_async_copy(target, outs[number], sem))
            stores[-1].start()
    for store in stores:
        store.wait()


def base_products(info, places, mine, other, groups, mp_count, kept, cover, *before):
    group_rows, features = mine.shape
    rows, span = group_rows // mp_count, groups[0][0].shape[1]
    wide = span * len(groups)
    shards = [shard for group in groups for shard in group]
    return pl.pallas_call(
        functools.partial(base_kernel, mp_count, [len(group) for group in groups], kept, places),
        in_specs=[SCALARS] + [WHOLE if kept else ANYWHERE] * 2 + [ANYWHERE] * (len(shards) + len(before)),
        out_specs=[ANYWHERE] * mp_count,
        scratch_shapes=[pltpu.VMEM((len(groups), features, span), mine.dtype)]
        + ([] if kept else [pltpu.VMEM((CORES * mp_count, rows, features), mine.dtype)])
        + [
            pltpu.VMEM((mp_count, CORES * rows, wide), jnp.bfloat16),
            pltpu.VMEM((CORES * rows, wide), jnp.float32),
            pltpu.SemaphoreType.DMA((len(groups) + (1 + CORES) * mp_count,)),
        ],
        out_shape=[
            jax.ShapeDtypeStruct((CORES * rows, wide), jnp.bfloat16 if number else jnp.float32)
            for number in range(mp_count)
        ],
        compiler_params=pltpu.CompilerParams(vmem_limit_bytes=VMEM_BYTES // 4 if kept else VMEM_BYTES),
        cost_estimate=cost(
            cover * 2 * CORES * group_rows * features * wide,
            2 * (CORES * group_rows * (features + wide) + features * wide),
        ),
    )(info, mine, other, *shards, *before)


def cut_down_kernel(info_ref, down_ref, out, block, sems):
    mp_count, features, lanes = block.shape
    mine = pl.ds(pl.multiple_of(info_ref[1] * lanes, lanes), lanes)
    loads = start_all(
        [(down_ref.at[n * features : (n + 1) * features, mine], block.at[n]) for n in range(mp_count)], sems
    )
    stores = []
    for n, load in enumerate(loads):
        load.wait()
        stores.append(pltpu.make_async_copy(block.at[n], out.at[n], sems.at[mp_count + n]))
        stores[-1].start()
    for store in stores:
        store.wait()


def cut_down(info, down, mp_count):
    shape = mp_count, down.shape[0] // mp_count, down.shape[1] // CORES
    return pl.pallas_call(
        cut_down_kernel,
        in_specs=[SCALARS, ANYWHERE],
        out_specs=ANYWHERE,
        out_shape=jax.ShapeDtypeStruct(shape, down.dtype),
        scratch_shapes=[pltpu.VMEM(shape, down.dtype), pltpu.SemaphoreType.DMA((2 * mp_count,))],
        compiler_params=pltpu.CompilerParams(vmem_limit_bytes=VMEM_BYTES // 6),
        cost_estimate=cost(0, 2 * down.size),
    )(info, down)


def cut_up_kernel(width, info_ref, up_ref, out, block, sems):
    parts, ranks, span = up_ref.shape
    lanes = block.shape[1]
    pairs = []
    for part in range(parts):
        for place in range(0, span, CORES * width):
            for first in range(place, place + width, lanes):
                columns = pl.ds(pl.multiple_of(first + info_ref[1] * width, lanes), lanes)
                row = len(pairs) * ranks
                pairs.append((up_ref.at[part, :, columns], block.at[row : row + ranks, :]))
    load_all(pairs, sems)
    load_all([(block, out.at[n]) for n in range(out.shape[0])], sems)


def cut_up(info, up, mp_count, width, lanes):
    parts, ranks, span = up.shape
    blocks = parts * span // CORES // lanes
    return pl.pallas_call(
        functools.partial(cut_up_kernel, width),
        in_specs=[SCALARS, ANYWHERE],
        out_specs=ANYWHERE,
        out_shape=jax.ShapeDtypeStruct((mp_count, blocks * ranks, lanes), up.dtype),
        scratch_shapes=[
            pltpu.VMEM((blocks * ranks, lanes), up.dtype),
            pltpu.SemaphoreType.DMA((max(blocks, mp_count),)),
        ],
        compiler_params=pltpu.CompilerParams(vmem_limit_bytes=VMEM_BYTES // 6),
        cost_estimate=cost(COVER * 2**32, 4 * mp_count * blocks * ranks * lanes),
    )(info, up)


def low_kernel(adapters, rank_pair, info_ref, mine_ref, other_ref, mine_ids, other_ids, maps_ref, _, out, maps, sems):
    mp_count, features, lanes = maps.shape
    rows = mine_ref.shape[0] // mp_count
    load_all([(maps_ref.at[number, :features, :], maps.at[number]) for number in range(mp_count)], sems)
    lane_adapter = lax.broadcasted_iota(jnp.int32, (rows, lanes), 1) // rank_pair
    groups = lanes // rank_pair
    depth = CORES * rows // groups
    lane_group = lax.broadcasted_iota(jnp.int32, (depth, lanes), 1) // rank_pair
    for number in range(mp_count):
        halves = []
        for part in range(CORES):
            place = slice(number * rows, (number + 1) * rows)
            ids = (mine_ids, other_ids)[part][place, :]
            values = (mine_ref, other_ref)[part][place, :]
            total = jnp.zeros((rows, lanes), jnp.float32)
            for owner in range(0, mp_count, CORES):
                both = jnp.concatenate([maps[owner], maps[owner + 1]], axis=1)
                product = jnp.dot(values, both, preferred_element_type=jnp.float32)
                for m in range(CORES):
                    wanted = ids - (owner + m) * adapters - info_ref[1] * groups
                    total += jnp.where(lane_adapter == wanted, product[:, m * lanes : (m + 1) * lanes], 0.0)
            shift = lanes // 2
            while shift >= rank_pair:
                total = total + pltpu.roll(total, shift, 1)
                shift //= 2
            halves.append(total)
        both = jnp.concatenate(halves, axis=0)
        packed = jnp.zeros((depth, lanes), jnp.float32)
        for group in range(groups):
            packed += jnp.where(lane_group == group, both[group * depth : (group + 1) * depth, :], 0.0)
        out[number] = packed


def low_sums(info, mine, other, ids, maps, adapters, rank, before):
    group_rows, features = mine.shape
    mp_count, _, lanes = maps.shape
    rows = group_rows // mp_count
    depth = CORES * rows * 2 * rank // lanes
    return pl.pallas_call(
        functools.partial(low_kernel, adapters, 2 * rank),
        in_specs=[SCALARS] + [WHOLE] * 4 + [ANYWHERE] * 2,
        out_specs=WHOLE,
        out_shape=jax.ShapeDtypeStruct((mp_count, depth, lanes), jnp.float32),
        scratch_shapes=[pltpu.VMEM((mp_count, features, lanes), maps.dtype), pltpu.SemaphoreType.DMA((mp_count,))],
        compiler_params=pltpu.CompilerParams(vmem_limit_bytes=VMEM_BYTES // 4),
        cost_estimate=cost(
            COVER * 2 * CORES * group_rows * features * mp_count * lanes,
            2 * features * (CORES * group_rows + mp_count * lanes)
        ),
    )(info, mine, other, *ids, maps, before)


def delta_kernel(adapters, rank, info_ref, mine_ids, other_ids, mine_ref, other_ref, maps_ref, out, maps, sem):
    copy = pltpu.make_async_copy(maps_ref.at[:, maps_ref.shape[1] - maps.shape[1] :, :], maps, sem)
    copy.start()
    mp_count = maps.shape[0]
    planes, rows, span = out.shape
    lanes = mine_ref.shape[2]
    rank_pair = 2 * rank
    groups = lanes // rank_pair
    depth = rows // groups
    packed = sum(mine_ref[n] for n in range(mp_count))
    packed = packed + pltpu.roll(sum(other_ref[n] for n in range(mp_count)), lanes // 2, 1)
    lane_group = lax.broadcasted_iota(jnp.int32, (depth, lanes), 1) // rank_pair
    spread = []
    for group in range(groups):
        values = jnp.where(lane_group == group, packed, 0.0)
        shift = lanes // 2
        while shift >= rank_pair:
            values = values + pltpu.roll(values, shift, 1)
            shift //= 2
        spread.append(values)
    low = jnp.concatenate(spread, axis=0)
    place = pl.ds(pl.multiple_of(info_ref[0] * (rows // CORES), rows // CORES), rows // CORES)
    ids = jnp.concatenate([mine_ids[place, :], other_ids[place, :]], axis=0)
    lane_block = lax.broadcasted_iota(jnp.int32, (rows, lanes), 1) // rank
    even = lane_block % 2 == 0
    lows = [jnp.where(even, low, pltpu.roll(low, rank, 1)), jnp.where(even, pltpu.roll(low, lanes - rank, 1), low)]
    copy.wait()
    ranks = adapters * rank
    for part in range(2):
        spreads = [
            jnp.where(lane_block == ids - owner * adapters, lows[part], 0.0).astype(jnp.bfloat16)
            for owner in range(mp_count)
        ]
        for plane in range(part * planes // 2, (part + 1) * planes // 2):
            for piece in range(span // lanes):
                first = (plane * (span // lanes) + piece) * ranks
                total = jnp.zeros((rows, lanes), jnp.float32)
                for owner in range(mp_count):
                    weights = maps[owner, first : first + ranks, :]
                    total += jnp.dot(spreads[owner], weights, preferred_element_type=jnp.float32)
                out[plane, :, piece * lanes : (piece + 1) * lanes] = (ADAPTER_SCALE * total).astype(out.dtype)


def deltas_of(info, ids, mine, other, maps, adapters, rank, planes, span):
    mp_count, _, lanes = maps.shape
    rows = CORES * ids[0].shape[0] // mp_count
    depth = planes * span // lanes * adapters * rank
    return pl.pallas_call(
        functools.partial(delta_kernel, adapters, rank),
        in_specs=[SCALARS] + [WHOLE] * 4 + [ANYWHERE],
        out_specs=WHOLE,
        out_shape=jax.ShapeDtypeStruct((planes, rows, span), jnp.bfloat16),
        scratch_shapes=[pltpu.VMEM((mp_count, depth, lanes), maps.dtype), pltpu.SemaphoreType.DMA],
        compiler_params=pltpu.CompilerParams(vmem_limit_bytes=VMEM_BYTES // 6),
        cost_estimate=cost(2 * rows * mp_count * depth * lanes, 2 * mp_count * depth * lanes),
    )(info, *ids, mine, other, maps)


def finish_kernel(mp_count, places, info_ref, delta_ref, *rest):
    parts, (out, away, delta, own, others, done, sems) = rest[:mp_count], rest[-7:]
    groups, rows, span = delta.shape
    rows //= CORES
    pairs = [(parts[0], own)] + [(part, others.at[n]) for n, part in enumerate(parts[1:])]
    pairs += [(delta_ref.at[info_ref[place]], delta.at[group]) for group, place in enumerate(places)]
    load_all(pairs, sems)
    pairs = [(done.at[rows:, :], away)]
    for group, place in enumerate(places):
        columns = slice(group * span, (group + 1) * span)
        total = own[:, columns]
        for n in range(mp_count - 1):
            total = total + others[n, :, columns].astype(jnp.float32)
        done[:, columns] = (total + delta[group].astype(jnp.float32)).astype(done.dtype)
        target = pl.ds(pl.multiple_of(info_ref[place + 1] * span, span), span)
        pairs.append((done.at[:rows, columns], out.at[:, target]))
    load_all(pairs, sems)


def finish(info, places, delta, parts, held, width):
    mp_count, groups = len(parts), len(places)
    rows, wide = parts[0].shape
    operands = [info, delta, *parts] + ([] if held is None else [held])
    return pl.pallas_call(
        functools.partial(finish_kernel, mp_count, places),
        in_specs=[SCALARS] + [ANYWHERE] * (len(operands) - 1),
        out_specs=[ANYWHERE] * 2,
        out_shape=[
            jax.ShapeDtypeStruct((rows // CORES, width), delta.dtype),
            jax.ShapeDtypeStruct((rows // CORES, wide), delta.dtype),
        ],
        scratch_shapes=[
            pltpu.VMEM((groups, rows, wide // groups), delta.dtype),
            pltpu.VMEM((rows, wide), jnp.float32),
            pltpu.VMEM((mp_count - 1, rows, wide), delta.dtype),
            pltpu.VMEM((rows, wide), delta.dtype),
            pltpu.SemaphoreType.DMA((mp_count + groups,)),
        ],
        input_output_aliases={} if held is None else {len(operands) - 1: 0},
        compiler_params=pltpu.CompilerParams(vmem_limit_bytes=VMEM_BYTES // 6),
        cost_estimate=cost(4 * rows * wide, 12 * rows * wide),
    )(*operands)


def settle_kernel(places, span, info_ref, *rest):
    pieces, (out, sems) = rest[: len(places)], rest[-2:]
    pairs = []
    for piece, some in zip(pieces, places):
        for group, place in enumerate(some):
            target = pl.ds(pl.multiple_of(info_ref[place] * span, span), span)
            pairs.append((piece.at[:, group * span : (group + 1) * span], out.at[:, target]))
    load_all(pairs, sems)


def settle(info, places, span, pieces, held):
    operands = [info, *pieces, held]
    return pl.pallas_call(
        functools.partial(settle_kernel, places, span),
        in_specs=[SCALARS] + [WHOLE] * len(pieces) + [ANYWHERE],
        out_specs=ANYWHERE,
        out_shape=jax.ShapeDtypeStruct(held.shape, held.dtype),
        scratch_shapes=[pltpu.SemaphoreType.DMA((sum(len(some) for some in places),))],
        input_output_aliases={len(operands) - 1: 0},
        compiler_params=pltpu.CompilerParams(vmem_limit_bytes=VMEM_BYTES // 6),
        cost_estimate=cost(0, 4 * sum(piece.size for piece in pieces)),
    )(*operands)


def by_plane(plane, values):
    return sum(jnp.where(plane == n, value, 0) for n, value in enumerate(values)).astype(jnp.int32)


def arrival_order(plane, planes):
    sides = (1, -1) if 2 * plane < planes else (-1, 1)
    return [
        (side, distance)
        for distance in range(1, planes)
        for side in sides
        if 0 <= plane + side * distance < planes
    ]


def local(tokens, frozen_weight, adapter_down_weight, adapter_up_weight, token_adapter_index):
    mp_count, dp_count = lax.axis_size("mp"), lax.axis_size("dp")
    position, replica = lax.axis_index("mp"), lax.axis_index("dp")
    planes = dp_count // CORES
    plane, core = replica // CORES, replica % CORES
    group_rows, features = tokens.shape
    rows = group_rows // mp_count
    width = frozen_weight.shape[1]
    adapters, rank, up_span = adapter_up_weight.shape[1:]
    ranks = adapters * rank

    def after_all(*arrays):
        return lax.optimization_barrier(arrays)

    def swap(array):
        return lax.ppermute(array, "dp", [(n, n ^ 1) for n in range(dp_count)])

    def trade(array):
        return lax.all_to_all(array, "mp", 0, 0)

    def pass_round(blocks):
        return [
            lax.ppermute(block, "mp", [(m, m ^ n) for m in range(mp_count)]) for n, block in enumerate(blocks, 1)
        ]

    def hop(array, side, step):
        sources = range(1, planes - step + 1) if side > 0 else range(step - 1, planes - 1)
        return lax.ppermute(
            array, "dp", [(CORES * n + m, CORES * (n - side) + m) for n in sources for m in range(CORES)]
        )

    got = {(side, 1): hop(frozen_weight, side, 1) for side in (1, -1)}
    other = swap(tokens)
    ids = token_adapter_index.reshape(group_rows, 1)
    ids = [ids, swap(token_adapter_index).reshape(group_rows, 1)]

    orders = [[(0, 0)] + arrival_order(n, planes) for n in range(planes)]
    options = [sorted({order[turn] for order in orders}) for turn in range(planes)]
    scalars = [position, core]
    choice_at, group_at = [], []
    for turn in range(planes):
        wanted = [order[turn] for order in orders]
        choice_at.append(len(scalars))
        scalars.append(by_plane(plane, [options[turn].index(item) for item in wanted]))
        group = by_plane(plane, [n + side * distance for n, (side, distance) in enumerate(wanted)])
        group_at.append(len(scalars))
        scalars += [group, CORES * group + core, CORES * group + 1 - core]
    info = jnp.stack([jnp.asarray(value, jnp.int32) for value in scalars])

    down = trade(cut_down(info, adapter_down_weight, mp_count))
    up = cut_up(info, adapter_up_weight.reshape(2, ranks, up_span), mp_count, width, down.shape[2])
    got[1, 1], got[-1, 1], up = after_all(got[1, 1], got[-1, 1], up)
    finished, places = [], []

    for turn in range(1, planes):
        last = turn == planes - 1
        if not last:
            if turn > 1:
                got[1, turn], got[-1, turn], own, sums = after_all(got[1, turn], got[-1, turn], own, sums)
            for side in (1, -1):
                got[side, turn + 1] = hop(got[side, turn], side, turn + 1)
        if turn > 1:
            finished.append([own] + pass_round(sent))
        before = []
        if last:
            delta = deltas_of(info, ids, sums, swap(sums), up, adapters, rank, planes, width)
            before = [delta]
        elif turn == 2:
            sums = trade(sums)
            up, sums = after_all(up, sums)
            up = trade(up)
            before = finished[0][1:]
        turns = [0, 1] if turn == 1 else [turn]
        groups = [[frozen_weight] if n == 0 else [got[option] for option in options[n]] for n in turns]
        kept = turn == 1 or last
        cover = 1 if turn == 1 else COVER
        own, *sent = base_products(
            info, [choice_at[n] for n in turns], tokens, other, groups, mp_count, kept, cover, *before
        )
        places.append([group_at[n] for n in turns])
        if turn == 1:
            sums = low_sums(info, tokens, other, ids, down, adapters, rank, own)
    finished.append([own] + pass_round(sent))

    out, away = None, []
    for some, parts in zip(places, finished):
        out, piece = finish(info, some, delta, parts, out, dp_count * width)
        away.append(swap(piece))
    places = [[place + 2 for place in some] for some in places]
    out = settle(info, places[:-1], width, away[:-1], out)
    return settle(info, places[-1:], width, away[-1:], out)


def solution(mesh):
    placed = (P("dp", "mp"), P("mp", "dp"), P(None, "mp"), P(None, "mp", None, None), P("dp"))
    return jax.shard_map(
        local, mesh=mesh, in_specs=placed, out_specs=P(("dp", "mp"), None), check_vma=False
    )
```

```python
import functools

import jax
import jax.numpy as jnp
from jax import lax
from jax.experimental import pallas as pl
from jax.experimental.pallas import tpu as pltpu
from jax.sharding import PartitionSpec as P

ADAPTER_SCALE = 2.0
CORES = 2
LANES = 128
COVER = 64
VMEM_BYTES = 60 * 1024 * 1024
ANYWHERE = pl.BlockSpec(memory_space=pl.ANY)
WHOLE = pl.BlockSpec(memory_space=pltpu.VMEM)
SCALARS = pl.BlockSpec(memory_space=pltpu.SMEM)


def params():
    return pltpu.CompilerParams(vmem_limit_bytes=VMEM_BYTES)


def cost(flops, bytes_accessed):
    return pl.CostEstimate(flops=flops, bytes_accessed=bytes_accessed, transcendentals=0)


def start_all(pairs, sems):
    copies = [pltpu.make_async_copy(src, dst, sems.at[n]) for n, (src, dst) in enumerate(pairs)]
    for copy in copies:
        copy.start()
    return copies


def load_all(pairs, sems):
    for copy in start_all(pairs, sems):
        copy.wait()


def base_kernel(mp_count, counts, kept, places, info_ref, mine_ref, other_ref, *rest):
    total = sum(counts)
    choices = rest[:total]
    weight, done, own, sems = rest[-4:] if kept else [*rest[-5:-4], *rest[-3:]]
    outs = rest[-4 - mp_count : -4] if kept else rest[-5 - mp_count : -5]
    rows = own.shape[0] // CORES
    span = weight.shape[2]
    first = 0
    for group, count in enumerate(counts):
        for number in range(count):

            @pl.when(info_ref[places[group]] == number)
            def _(group=group, choice=choices[first + number]):
                pltpu.make_async_copy(choice, weight.at[group], sems.at[group]).start()

        first += count

    order = [(number, part) for number in reversed(range(mp_count)) for part in range(CORES)]
    blocks, copies = {}, []
    for number, part in order:
        place = pl.ds(pl.multiple_of((info_ref[0] ^ number) * rows, rows), rows)
        source = (mine_ref, other_ref)[part].at[place, :]
        n = CORES * number + part
        blocks[n] = source if kept else rest[-4].at[n]
        if not kept:
            copies.append(pltpu.make_async_copy(source, blocks[n], sems.at[len(counts) + n]))
            copies[-1].start()
    for group in range(len(counts)):
        pltpu.make_async_copy(choices[0], weight.at[group], sems.at[group]).wait()
    stores = []
    for turn, (number, part) in enumerate(order):
        if not kept:
            copies[turn].wait()
        target = done.at[number] if number else own
        for group in range(len(counts)):
            product = jnp.dot(
                blocks[CORES * number + part][...], weight[group], preferred_element_type=jnp.float32
            )
            columns = slice(group * span, (group + 1) * span)
            target[part * rows : (part + 1) * rows, columns] = product.astype(target.dtype)
        if part:
            sem = sems.at[len(counts) + CORES * mp_count + number]
            stores.append(pltpu.make_async_copy(target, outs[number], sem))
            stores[-1].start()
    for store in stores:
        store.wait()


def base_products(info, places, mine, other, groups, mp_count, kept, cover, *before):
    group_rows, features = mine.shape
    rows, span = group_rows // mp_count, groups[0][0].shape[1]
    wide = span * len(groups)
    shards = [shard for group in groups for shard in group]
    return pl.pallas_call(
        functools.partial(base_kernel, mp_count, [len(group) for group in groups], kept, places),
        in_specs=[SCALARS] + [WHOLE if kept else ANYWHERE] * 2 + [ANYWHERE] * (len(shards) + len(before)),
        out_specs=[ANYWHERE] * mp_count,
        scratch_shapes=[pltpu.VMEM((len(groups), features, span), mine.dtype)]
        + ([] if kept else [pltpu.VMEM((CORES * mp_count, rows, features), mine.dtype)])
        + [
            pltpu.VMEM((mp_count, CORES * rows, wide), jnp.bfloat16),
            pltpu.VMEM((CORES * rows, wide), jnp.float32),
            pltpu.SemaphoreType.DMA((len(groups) + (1 + CORES) * mp_count,)),
        ],
        out_shape=[
            jax.ShapeDtypeStruct((CORES * rows, wide), jnp.bfloat16 if number else jnp.float32)
            for number in range(mp_count)
        ],
        compiler_params=pltpu.CompilerParams(vmem_limit_bytes=VMEM_BYTES // 4 if kept else VMEM_BYTES),
        cost_estimate=cost(
            cover * 2 * CORES * group_rows * features * wide,
            2 * (CORES * group_rows * (features + wide) + features * wide),
        ),
    )(info, mine, other, *shards, *before)


def cut_down_kernel(info_ref, down_ref, out, block, sems):
    mp_count, features, lanes = block.shape
    mine = pl.ds(pl.multiple_of(info_ref[1] * lanes, lanes), lanes)
    loads = start_all(
        [(down_ref.at[n * features : (n + 1) * features, mine], block.at[n]) for n in range(mp_count)], sems
    )
    stores = []
    for n, load in enumerate(loads):
        load.wait()
        stores.append(pltpu.make_async_copy(block.at[n], out.at[n], sems.at[mp_count + n]))
        stores[-1].start()
    for store in stores:
        store.wait()


def cut_down(info, down, mp_count):
    shape = mp_count, down.shape[0] // mp_count, down.shape[1] // CORES
    return pl.pallas_call(
        cut_down_kernel,
        in_specs=[SCALARS, ANYWHERE],
        out_specs=ANYWHERE,
        out_shape=jax.ShapeDtypeStruct(shape, down.dtype),
        scratch_shapes=[pltpu.VMEM(shape, down.dtype), pltpu.SemaphoreType.DMA((2 * mp_count,))],
        compiler_params=pltpu.CompilerParams(vmem_limit_bytes=VMEM_BYTES // 6),
        cost_estimate=cost(0, 2 * down.size),
    )(info, down)


def cut_up_kernel(width, info_ref, up_ref, out, block, sems):
    parts, ranks, span = up_ref.shape
    lanes = block.shape[1]
    pairs = []
    for part in range(parts):
        for place in range(0, span, CORES * width):
            for first in range(place, place + width, lanes):
                columns = pl.ds(pl.multiple_of(first + info_ref[1] * width, lanes), lanes)
                row = len(pairs) * ranks
                pairs.append((up_ref.at[part, :, columns], block.at[row : row + ranks, :]))
    load_all(pairs, sems)
    load_all([(block, out.at[n]) for n in range(out.shape[0])], sems)


def cut_up(info, up, mp_count, width, lanes):
    parts, ranks, span = up.shape
    blocks = parts * span // CORES // lanes
    return pl.pallas_call(
        functools.partial(cut_up_kernel, width),
        in_specs=[SCALARS, ANYWHERE],
        out_specs=ANYWHERE,
        out_shape=jax.ShapeDtypeStruct((mp_count, blocks * ranks, lanes), up.dtype),
        scratch_shapes=[
            pltpu.VMEM((blocks * ranks, lanes), up.dtype),
            pltpu.SemaphoreType.DMA((max(blocks, mp_count),)),
        ],
        compiler_params=pltpu.CompilerParams(vmem_limit_bytes=VMEM_BYTES // 6),
        cost_estimate=cost(COVER * 2**32, 4 * mp_count * blocks * ranks * lanes),
    )(info, up)


def low_kernel(adapters, rank_pair, info_ref, mine_ref, other_ref, mine_ids, other_ids, maps_ref, _, out, maps, sems):
    mp_count, features, lanes = maps.shape
    rows = mine_ref.shape[0] // mp_count
    load_all([(maps_ref.at[number, :features, :], maps.at[number]) for number in range(mp_count)], sems)
    lane_adapter = lax.broadcasted_iota(jnp.int32, (rows, lanes), 1) // rank_pair
    groups = lanes // rank_pair
    depth = CORES * rows // groups
    lane_group = lax.broadcasted_iota(jnp.int32, (depth, lanes), 1) // rank_pair
    for number in range(mp_count):
        halves = []
        for part in range(CORES):
            place = slice(number * rows, (number + 1) * rows)
            ids = (mine_ids, other_ids)[part][place, :]
            values = (mine_ref, other_ref)[part][place, :]
            total = jnp.zeros((rows, lanes), jnp.float32)
            for owner in range(0, mp_count, CORES):
                both = jnp.concatenate([maps[owner], maps[owner + 1]], axis=1)
                product = jnp.dot(values, both, preferred_element_type=jnp.float32)
                for m in range(CORES):
                    wanted = ids - (owner + m) * adapters - info_ref[1] * groups
                    total += jnp.where(lane_adapter == wanted, product[:, m * lanes : (m + 1) * lanes], 0.0)
            shift = lanes // 2
            while shift >= rank_pair:
                total = total + pltpu.roll(total, shift, 1)
                shift //= 2
            halves.append(total)
        both = jnp.concatenate(halves, axis=0)
        packed = jnp.zeros((depth, lanes), jnp.float32)
        for group in range(groups):
            packed += jnp.where(lane_group == group, both[group * depth : (group + 1) * depth, :], 0.0)
        out[number] = packed


def low_sums(info, mine, other, ids, maps, adapters, rank, before):
    group_rows, features = mine.shape
    mp_count, _, lanes = maps.shape
    rows = group_rows // mp_count
    depth = CORES * rows * 2 * rank // lanes
    return pl.pallas_call(
        functools.partial(low_kernel, adapters, 2 * rank),
        in_specs=[SCALARS] + [WHOLE] * 4 + [ANYWHERE] * 2,
        out_specs=WHOLE,
        out_shape=jax.ShapeDtypeStruct((mp_count, depth, lanes), jnp.float32),
        scratch_shapes=[pltpu.VMEM((mp_count, features, lanes), maps.dtype), pltpu.SemaphoreType.DMA((mp_count,))],
        compiler_params=pltpu.CompilerParams(vmem_limit_bytes=VMEM_BYTES // 4),
        cost_estimate=cost(
            COVER * 2 * CORES * group_rows * features * mp_count * lanes,
            2 * features * (CORES * group_rows + mp_count * lanes)
        ),
    )(info, mine, other, *ids, maps, before)


def delta_kernel(adapters, rank, info_ref, mine_ids, other_ids, mine_ref, other_ref, maps_ref, out, maps, sem):
    mp_count, _, lanes = maps_ref.shape
    planes, rows, span = out.shape
    ranks = adapters * rank
    copies = []
    for plane in range(planes):
        for first in range(0, span, lanes):
            row = (plane * span + first) // lanes * ranks
            for owner in range(mp_count):
                target = maps.at[plane, owner * ranks : (owner + 1) * ranks, first : first + lanes]
                copies.append(pltpu.make_async_copy(maps_ref.at[owner, row : row + ranks, :], target, sem))
                copies[-1].start()
    rank_pair = 2 * rank
    groups = lanes // rank_pair
    depth = rows // groups
    packed = sum(mine_ref[n] for n in range(mp_count))
    packed = packed + pltpu.roll(sum(other_ref[n] for n in range(mp_count)), lanes // 2, 1)
    lane_group = lax.broadcasted_iota(jnp.int32, (depth, lanes), 1) // rank_pair
    spread = []
    for group in range(groups):
        values = jnp.where(lane_group == group, packed, 0.0)
        shift = lanes // 2
        while shift >= rank_pair:
            values = values + pltpu.roll(values, shift, 1)
            shift //= 2
        spread.append(values)
    low = jnp.concatenate(spread, axis=0)
    place = pl.ds(pl.multiple_of(info_ref[0] * (rows // CORES), rows // CORES), rows // CORES)
    ids = jnp.concatenate([mine_ids[place, :], other_ids[place, :]], axis=0)
    lane_block = lax.broadcasted_iota(jnp.int32, (rows, lanes), 1) // rank
    even = lane_block % 2 == 0
    lows = [jnp.where(even, low, pltpu.roll(low, rank, 1)), jnp.where(even, pltpu.roll(low, lanes - rank, 1), low)]
    for copy in copies:
        copy.wait()
    for part in range(2):
        spread = jnp.concatenate(
            [
                jnp.where(lane_block == ids - owner * adapters, lows[part], 0.0).astype(jnp.bfloat16)
                for owner in range(mp_count)
            ],
            axis=1,
        )
        for plane in range(part * planes // 2, (part + 1) * planes // 2):
            total = jnp.dot(spread, maps[plane], preferred_element_type=jnp.float32)
            out[plane] = (ADAPTER_SCALE * total).astype(out.dtype)


def deltas_of(info, ids, mine, other, maps, adapters, rank, planes, span):
    mp_count, _, lanes = maps.shape
    rows = CORES * ids[0].shape[0] // mp_count
    depth = mp_count * adapters * rank
    return pl.pallas_call(
        functools.partial(delta_kernel, adapters, rank),
        in_specs=[SCALARS] + [WHOLE] * 4 + [ANYWHERE],
        out_specs=WHOLE,
        out_shape=jax.ShapeDtypeStruct((planes, rows, span), jnp.bfloat16),
        scratch_shapes=[pltpu.VMEM((planes, depth, span), maps.dtype), pltpu.SemaphoreType.DMA],
        compiler_params=pltpu.CompilerParams(vmem_limit_bytes=VMEM_BYTES // 6),
        cost_estimate=cost(2 * rows * planes * depth * span, 2 * planes * depth * span),
    )(info, *ids, mine, other, maps)


def finish_kernel(mp_count, places, info_ref, delta_ref, *rest):
    turns = len(places)
    parts, scratch = rest[: mp_count * turns], rest[-1 - 4 * turns :]
    out, away = rest[-3 - 4 * turns : -1 - 4 * turns]
    sems = scratch[-1]
    rows = away.shape[0]
    pairs = []
    for turn, some in enumerate(places):
        delta, own, others, _ = scratch[4 * turn : 4 * turn + 4]
        first, *peers = parts[mp_count * turn : mp_count * (turn + 1)]
        pairs += [(first, own)] + [(part, others.at[n]) for n, part in enumerate(peers)]
        pairs += [(delta_ref.at[info_ref[place]], delta.at[group]) for group, place in enumerate(some)]
    load_all(pairs, sems)
    pairs, at = [], 0
    for turn, some in enumerate(places):
        delta, own, others, done = scratch[4 * turn : 4 * turn + 4]
        span = delta.shape[2]
        for group, place in enumerate(some):
            columns = slice(group * span, (group + 1) * span)
            total = own[:, columns]
            for n in range(mp_count - 1):
                total = total + others[n, :, columns].astype(jnp.float32)
            done[:, columns] = (total + delta[group].astype(jnp.float32)).astype(done.dtype)
            target = pl.ds(pl.multiple_of(info_ref[place + 1] * span, span), span)
            pairs.append((done.at[rows:, columns], away.at[:, at : at + span]))
            pairs.append((done.at[:rows, columns], out.at[:, target]))
            at += span
    load_all(pairs, sems)


def finish(info, places, delta, parts, held, width, *before):
    mp_count, rows = len(parts[0]), parts[0][0].shape[0]
    span = delta.shape[2]
    count = sum(len(some) for some in places)
    operands = [info, delta, *sum(parts, []), *before] + ([] if held is None else [held])
    scratch = []
    for some in places:
        wide = span * len(some)
        scratch += [
            pltpu.VMEM((len(some), rows, span), delta.dtype),
            pltpu.VMEM((rows, wide), jnp.float32),
            pltpu.VMEM((mp_count - 1, rows, wide), delta.dtype),
            pltpu.VMEM((rows, wide), delta.dtype),
        ]
    held_bytes = rows * span * count * (2 * mp_count + 6)
    return pl.pallas_call(
        functools.partial(finish_kernel, mp_count, places),
        in_specs=[SCALARS] + [ANYWHERE] * (len(operands) - 1),
        out_specs=[ANYWHERE] * 2,
        out_shape=[
            jax.ShapeDtypeStruct((rows // CORES, width), delta.dtype),
            jax.ShapeDtypeStruct((rows // CORES, span * count), delta.dtype),
        ],
        scratch_shapes=scratch + [pltpu.SemaphoreType.DMA((mp_count * len(places) + 2 * count,))],
        input_output_aliases={} if held is None else {len(operands) - 1: 0},
        compiler_params=pltpu.CompilerParams(vmem_limit_bytes=VMEM_BYTES // 10 + held_bytes + held_bytes // 4),
        cost_estimate=cost(4 * rows * span * count, 12 * rows * span * count),
    )(*operands)


def settle_kernel(places, span, info_ref, *rest):
    pieces, (out, sems) = rest[: len(places)], rest[-2:]
    pairs = []
    for piece, some in zip(pieces, places):
        for group, place in enumerate(some):
            target = pl.ds(pl.multiple_of(info_ref[place] * span, span), span)
            pairs.append((piece.at[:, group * span : (group + 1) * span], out.at[:, target]))
    load_all(pairs, sems)


def settle(info, places, span, pieces, held):
    operands = [info, *pieces, held]
    return pl.pallas_call(
        functools.partial(settle_kernel, places, span),
        in_specs=[SCALARS] + [WHOLE] * len(pieces) + [ANYWHERE],
        out_specs=ANYWHERE,
        out_shape=jax.ShapeDtypeStruct(held.shape, held.dtype),
        scratch_shapes=[pltpu.SemaphoreType.DMA((sum(len(some) for some in places),))],
        input_output_aliases={len(operands) - 1: 0},
        compiler_params=pltpu.CompilerParams(vmem_limit_bytes=VMEM_BYTES // 6),
        cost_estimate=cost(0, 4 * sum(piece.size for piece in pieces)),
    )(*operands)


def by_plane(plane, values):
    return sum(jnp.where(plane == n, value, 0) for n, value in enumerate(values)).astype(jnp.int32)


def arrival_order(plane, planes):
    sides = (1, -1) if 2 * plane < planes else (-1, 1)
    return [
        (side, distance)
        for distance in range(1, planes)
        for side in sides
        if 0 <= plane + side * distance < planes
    ]


def local(tokens, frozen_weight, adapter_down_weight, adapter_up_weight, token_adapter_index):
    mp_count, dp_count = lax.axis_size("mp"), lax.axis_size("dp")
    position, replica = lax.axis_index("mp"), lax.axis_index("dp")
    planes = dp_count // CORES
    plane, core = replica // CORES, replica % CORES
    group_rows, features = tokens.shape
    rows = group_rows // mp_count
    width = frozen_weight.shape[1]
    adapters, rank, up_span = adapter_up_weight.shape[1:]
    ranks = adapters * rank

    def after_all(*arrays):
        return lax.optimization_barrier(arrays)

    def swap(array):
        return lax.ppermute(array, "dp", [(n, n ^ 1) for n in range(dp_count)])

    def trade(array):
        return lax.all_to_all(array, "mp", 0, 0)

    def pass_round(blocks):
        return [
            lax.ppermute(block, "mp", [(m, m ^ n) for m in range(mp_count)]) for n, block in enumerate(blocks, 1)
        ]

    def hop(array, side, step):
        sources = range(1, planes - step + 1) if side > 0 else range(step - 1, planes - 1)
        return lax.ppermute(
            array, "dp", [(CORES * n + m, CORES * (n - side) + m) for n in sources for m in range(CORES)]
        )

    got = {(side, 1): hop(frozen_weight, side, 1) for side in (1, -1)}
    other = swap(tokens)
    ids = token_adapter_index.reshape(group_rows, 1)
    ids = [ids, swap(token_adapter_index).reshape(group_rows, 1)]

    orders = [[(0, 0)] + arrival_order(n, planes) for n in range(planes)]
    options = [sorted({order[turn] for order in orders}) for turn in range(planes)]
    scalars = [position, core]
    choice_at, group_at = [], []
    for turn in range(planes):
        wanted = [order[turn] for order in orders]
        choice_at.append(len(scalars))
        scalars.append(by_plane(plane, [options[turn].index(item) for item in wanted]))
        group = by_plane(plane, [n + side * distance for n, (side, distance) in enumerate(wanted)])
        group_at.append(len(scalars))
        scalars += [group, CORES * group + core, CORES * group + 1 - core]
    info = jnp.stack([jnp.asarray(value, jnp.int32) for value in scalars])

    down = trade(cut_down(info, adapter_down_weight, mp_count))
    up = cut_up(info, adapter_up_weight.reshape(2, ranks, up_span), mp_count, width, down.shape[2])
    got[1, 1], got[-1, 1], up = after_all(got[1, 1], got[-1, 1], up)
    finished, places = [], []

    for turn in range(1, planes):
        last = turn == planes - 1
        if not last:
            if turn > 1:
                got[1, turn], got[-1, turn], own, sums = after_all(got[1, turn], got[-1, turn], own, sums)
            for side in (1, -1):
                got[side, turn + 1] = hop(got[side, turn], side, turn + 1)
        if turn > 1:
            finished.append([own] + pass_round(sent))
        before = []
        if last:
            delta = deltas_of(info, ids, sums, swap(sums), up, adapters, rank, planes, width)
            before = [delta]
        elif turn == 2:
            sums = trade(sums)
            up, sums = after_all(up, sums)
            up = trade(up)
            before = finished[0][1:]
        turns = [0, 1] if turn == 1 else [turn]
        groups = [[frozen_weight] if n == 0 else [got[option] for option in options[n]] for n in turns]
        kept = turn == 1 or last
        cover = 1 if turn == 1 else COVER
        own, *sent = base_products(
            info, [choice_at[n] for n in turns], tokens, other, groups, mp_count, kept, cover, *before
        )
        places.append([group_at[n] for n in turns])
        if turn == 1:
            sums = low_sums(info, tokens, other, ids, down, adapters, rank, own)
    finished.append([own] + pass_round(sent))

    out, first = finish(info, places[:-1], delta, finished[:-1], None, dp_count * width, own)
    first = swap(first)
    out, second = finish(info, places[-1:], delta, finished[-1:], out, dp_count * width)
    second = swap(second)
    places = [place + 2 for some in places for place in some]
    out = settle(info, [places[:-1]], width, [first], out)
    return settle(info, [places[-1:]], width, [second], out)


def solution(mesh):
    placed = (P("dp", "mp"), P("mp", "dp"), P(None, "mp"), P(None, "mp", None, None), P("dp"))
    return jax.shard_map(
        local, mesh=mesh, in_specs=placed, out_specs=P(("dp", "mp"), None), check_vma=False
    )
```

```python
import functools

import jax
import jax.numpy as jnp
from jax import lax
from jax.experimental import pallas as pl
from jax.experimental.pallas import tpu as pltpu
from jax.sharding import PartitionSpec as P

ADAPTER_SCALE = 2.0
CORES = 2
LANES = 128
COVER = 64
VMEM_BYTES = 60 * 1024 * 1024
ANYWHERE = pl.BlockSpec(memory_space=pl.ANY)
WHOLE = pl.BlockSpec(memory_space=pltpu.VMEM)
SCALARS = pl.BlockSpec(memory_space=pltpu.SMEM)


def params():
    return pltpu.CompilerParams(vmem_limit_bytes=VMEM_BYTES)


def cost(flops, bytes_accessed):
    return pl.CostEstimate(flops=flops, bytes_accessed=bytes_accessed, transcendentals=0)


def start_all(pairs, sems):
    copies = [pltpu.make_async_copy(src, dst, sems.at[n]) for n, (src, dst) in enumerate(pairs)]
    for copy in copies:
        copy.start()
    return copies


def load_all(pairs, sems):
    for copy in start_all(pairs, sems):
        copy.wait()


def base_kernel(mp_count, counts, kept, places, info_ref, mine_ref, other_ref, *rest):
    total = sum(counts)
    choices = rest[:total]
    weight, done, own, sems = rest[-4:] if kept else [*rest[-5:-4], *rest[-3:]]
    outs = rest[-4 - mp_count : -4] if kept else rest[-5 - mp_count : -5]
    rows = own.shape[0] // CORES
    span = weight.shape[2]
    first = 0
    for group, count in enumerate(counts):
        for number in range(count):

            @pl.when(info_ref[places[group]] == number)
            def _(group=group, choice=choices[first + number]):
                pltpu.make_async_copy(choice, weight.at[group], sems.at[group]).start()

        first += count

    order = [(number, part) for number in reversed(range(mp_count)) for part in range(CORES)]
    blocks, copies = {}, []
    for number, part in order:
        place = pl.ds(pl.multiple_of((info_ref[0] ^ number) * rows, rows), rows)
        source = (mine_ref, other_ref)[part].at[place, :]
        n = CORES * number + part
        blocks[n] = source if kept else rest[-4].at[n]
        if not kept:
            copies.append(pltpu.make_async_copy(source, blocks[n], sems.at[len(counts) + n]))
            copies[-1].start()
    for group in range(len(counts)):
        pltpu.make_async_copy(choices[0], weight.at[group], sems.at[group]).wait()
    stores = []
    for turn, (number, part) in enumerate(order):
        if not kept:
            copies[turn].wait()
        target = done.at[number] if number else own
        for group in range(len(counts)):
            product = jnp.dot(
                blocks[CORES * number + part][...], weight[group], preferred_element_type=jnp.float32
            )
            columns = slice(group * span, (group + 1) * span)
            target[part * rows : (part + 1) * rows, columns] = product.astype(target.dtype)
        if part:
            sem = sems.at[len(counts) + CORES * mp_count + number]
            stores.append(pltpu.make_async_copy(target, outs[number], sem))
            stores[-1].start()
    for store in stores:
        store.wait()


def base_products(info, places, mine, other, groups, mp_count, kept, cover, *before):
    group_rows, features = mine.shape
    rows, span = group_rows // mp_count, groups[0][0].shape[1]
    wide = span * len(groups)
    shards = [shard for group in groups for shard in group]
    return pl.pallas_call(
        functools.partial(base_kernel, mp_count, [len(group) for group in groups], kept, places),
        in_specs=[SCALARS] + [WHOLE if kept else ANYWHERE] * 2 + [ANYWHERE] * (len(shards) + len(before)),
        out_specs=[ANYWHERE] * mp_count,
        scratch_shapes=[pltpu.VMEM((len(groups), features, span), mine.dtype)]
        + ([] if kept else [pltpu.VMEM((CORES * mp_count, rows, features), mine.dtype)])
        + [
            pltpu.VMEM((mp_count, CORES * rows, wide), jnp.bfloat16),
            pltpu.VMEM((CORES * rows, wide), jnp.float32),
            pltpu.SemaphoreType.DMA((len(groups) + (1 + CORES) * mp_count,)),
        ],
        out_shape=[
            jax.ShapeDtypeStruct((CORES * rows, wide), jnp.bfloat16 if number else jnp.float32)
            for number in range(mp_count)
        ],
        compiler_params=pltpu.CompilerParams(vmem_limit_bytes=VMEM_BYTES // 4 if kept else VMEM_BYTES),
        cost_estimate=cost(
            cover * 2 * CORES * group_rows * features * wide,
            2 * (CORES * group_rows * (features + wide) + features * wide),
        ),
    )(info, mine, other, *shards, *before)


def cut_down_kernel(info_ref, down_ref, out, block, sems):
    mp_count, features, lanes = block.shape
    mine = pl.ds(pl.multiple_of(info_ref[1] * lanes, lanes), lanes)
    loads = start_all(
        [(down_ref.at[n * features : (n + 1) * features, mine], block.at[n]) for n in range(mp_count)], sems
    )
    stores = []
    for n, load in enumerate(loads):
        load.wait()
        stores.append(pltpu.make_async_copy(block.at[n], out.at[n], sems.at[mp_count + n]))
        stores[-1].start()
    for store in stores:
        store.wait()


def cut_down(info, down, mp_count):
    shape = mp_count, down.shape[0] // mp_count, down.shape[1] // CORES
    return pl.pallas_call(
        cut_down_kernel,
        in_specs=[SCALARS, ANYWHERE],
        out_specs=ANYWHERE,
        out_shape=jax.ShapeDtypeStruct(shape, down.dtype),
        scratch_shapes=[pltpu.VMEM(shape, down.dtype), pltpu.SemaphoreType.DMA((2 * mp_count,))],
        compiler_params=pltpu.CompilerParams(vmem_limit_bytes=VMEM_BYTES // 6),
        cost_estimate=cost(0, 2 * down.size),
    )(info, down)


def cut_up_kernel(width, info_ref, up_ref, out, block, sems):
    parts, ranks, span = up_ref.shape
    lanes = block.shape[1]
    pairs = []
    for part in range(parts):
        for place in range(0, span, CORES * width):
            for first in range(place, place + width, lanes):
                columns = pl.ds(pl.multiple_of(first + info_ref[1] * width, lanes), lanes)
                row = len(pairs) * ranks
                pairs.append((up_ref.at[part, :, columns], block.at[row : row + ranks, :]))
    load_all(pairs, sems)
    load_all([(block, out.at[n]) for n in range(out.shape[0])], sems)


def cut_up(info, up, mp_count, width, lanes):
    parts, ranks, span = up.shape
    blocks = parts * span // CORES // lanes
    return pl.pallas_call(
        functools.partial(cut_up_kernel, width),
        in_specs=[SCALARS, ANYWHERE],
        out_specs=ANYWHERE,
        out_shape=jax.ShapeDtypeStruct((mp_count, blocks * ranks, lanes), up.dtype),
        scratch_shapes=[
            pltpu.VMEM((blocks * ranks, lanes), up.dtype),
            pltpu.SemaphoreType.DMA((max(blocks, mp_count),)),
        ],
        compiler_params=pltpu.CompilerParams(vmem_limit_bytes=VMEM_BYTES // 6),
        cost_estimate=cost(COVER * 2**32, 4 * mp_count * blocks * ranks * lanes),
    )(info, up)


def low_kernel(adapters, rank_pair, info_ref, mine_ref, other_ref, mine_ids, other_ids, maps_ref, _, out, maps, sems):
    mp_count, features, lanes = maps.shape
    rows = mine_ref.shape[0] // mp_count
    load_all([(maps_ref.at[number, :features, :], maps.at[number]) for number in range(mp_count)], sems)
    lane_adapter = lax.broadcasted_iota(jnp.int32, (rows, lanes), 1) // rank_pair
    groups = lanes // rank_pair
    depth = CORES * rows // groups
    lane_group = lax.broadcasted_iota(jnp.int32, (depth, lanes), 1) // rank_pair
    for number in range(mp_count):
        halves = []
        for part in range(CORES):
            place = slice(number * rows, (number + 1) * rows)
            ids = (mine_ids, other_ids)[part][place, :]
            values = (mine_ref, other_ref)[part][place, :]
            total = jnp.zeros((rows, lanes), jnp.float32)
            for owner in range(0, mp_count, CORES):
                both = jnp.concatenate([maps[owner], maps[owner + 1]], axis=1)
                product = jnp.dot(values, both, preferred_element_type=jnp.float32)
                for m in range(CORES):
                    wanted = ids - (owner + m) * adapters - info_ref[1] * groups
                    total += jnp.where(lane_adapter == wanted, product[:, m * lanes : (m + 1) * lanes], 0.0)
            shift = lanes // 2
            while shift >= rank_pair:
                total = total + pltpu.roll(total, shift, 1)
                shift //= 2
            halves.append(total)
        both = jnp.concatenate(halves, axis=0)
        packed = jnp.zeros((depth, lanes), jnp.float32)
        for group in range(groups):
            packed += jnp.where(lane_group == group, both[group * depth : (group + 1) * depth, :], 0.0)
        out[number] = packed


def low_sums(info, mine, other, ids, maps, adapters, rank, before):
    group_rows, features = mine.shape
    mp_count, _, lanes = maps.shape
    rows = group_rows // mp_count
    depth = CORES * rows * 2 * rank // lanes
    return pl.pallas_call(
        functools.partial(low_kernel, adapters, 2 * rank),
        in_specs=[SCALARS] + [WHOLE] * 4 + [ANYWHERE] * 2,
        out_specs=WHOLE,
        out_shape=jax.ShapeDtypeStruct((mp_count, depth, lanes), jnp.float32),
        scratch_shapes=[pltpu.VMEM((mp_count, features, lanes), maps.dtype), pltpu.SemaphoreType.DMA((mp_count,))],
        compiler_params=pltpu.CompilerParams(vmem_limit_bytes=VMEM_BYTES // 4),
        cost_estimate=cost(
            COVER * 2 * CORES * group_rows * features * mp_count * lanes,
            2 * features * (CORES * group_rows + mp_count * lanes)
        ),
    )(info, mine, other, *ids, maps, before)


def delta_kernel(adapters, rank, info_ref, mine_ids, other_ids, mine_ref, other_ref, maps_ref, out, maps, sem):
    mp_count, _, lanes = maps_ref.shape
    planes, rows, span = out.shape
    ranks = adapters * rank
    copies = []
    for plane in range(planes):
        for first in range(0, span, lanes):
            row = (plane * span + first) // lanes * ranks
            for owner in range(mp_count):
                target = maps.at[plane, owner * ranks : (owner + 1) * ranks, first : first + lanes]
                copies.append(pltpu.make_async_copy(maps_ref.at[owner, row : row + ranks, :], target, sem))
                copies[-1].start()
    rank_pair = 2 * rank
    groups = lanes // rank_pair
    depth = rows // groups
    packed = sum(mine_ref[n] for n in range(mp_count))
    packed = packed + pltpu.roll(sum(other_ref[n] for n in range(mp_count)), lanes // 2, 1)
    lane_group = lax.broadcasted_iota(jnp.int32, (depth, lanes), 1) // rank_pair
    spread = []
    for group in range(groups):
        values = jnp.where(lane_group == group, packed, 0.0)
        shift = lanes // 2
        while shift >= rank_pair:
            values = values + pltpu.roll(values, shift, 1)
            shift //= 2
        spread.append(values)
    low = jnp.concatenate(spread, axis=0)
    place = pl.ds(pl.multiple_of(info_ref[0] * (rows // CORES), rows // CORES), rows // CORES)
    ids = jnp.concatenate([mine_ids[place, :], other_ids[place, :]], axis=0)
    lane_block = lax.broadcasted_iota(jnp.int32, (rows, lanes), 1) // rank
    even = lane_block % 2 == 0
    lows = [jnp.where(even, low, pltpu.roll(low, rank, 1)), jnp.where(even, pltpu.roll(low, lanes - rank, 1), low)]
    for copy in copies:
        copy.wait()
    for part in range(2):
        spread = jnp.concatenate(
            [
                jnp.where(lane_block == ids - owner * adapters, lows[part], 0.0).astype(jnp.bfloat16)
                for owner in range(mp_count)
            ],
            axis=1,
        )
        for plane in range(part * planes // 2, (part + 1) * planes // 2):
            total = jnp.dot(spread, maps[plane], preferred_element_type=jnp.float32)
            out[plane] = (ADAPTER_SCALE * total).astype(out.dtype)


def deltas_of(info, ids, mine, other, maps, adapters, rank, planes, span):
    mp_count, _, lanes = maps.shape
    rows = CORES * ids[0].shape[0] // mp_count
    depth = mp_count * adapters * rank
    return pl.pallas_call(
        functools.partial(delta_kernel, adapters, rank),
        in_specs=[SCALARS] + [WHOLE] * 4 + [ANYWHERE],
        out_specs=WHOLE,
        out_shape=jax.ShapeDtypeStruct((planes, rows, span), jnp.bfloat16),
        scratch_shapes=[pltpu.VMEM((planes, depth, span), maps.dtype), pltpu.SemaphoreType.DMA],
        compiler_params=pltpu.CompilerParams(vmem_limit_bytes=VMEM_BYTES // 6),
        cost_estimate=cost(2 * rows * planes * depth * span, 2 * planes * depth * span),
    )(info, *ids, mine, other, maps)


def finish_kernel(mp_count, places, info_ref, delta_ref, *rest):
    turns = len(places)
    parts, scratch = rest[: mp_count * turns], rest[-1 - 4 * turns :]
    out, away = rest[-3 - 4 * turns : -1 - 4 * turns]
    sems = scratch[-1]
    rows = away.shape[0]
    pairs = []
    for turn, some in enumerate(places):
        delta, own, others, _ = scratch[4 * turn : 4 * turn + 4]
        first, *peers = parts[mp_count * turn : mp_count * (turn + 1)]
        pairs += [(first, own)] + [(part, others.at[n]) for n, part in enumerate(peers)]
        pairs += [(delta_ref.at[info_ref[place]], delta.at[group]) for group, place in enumerate(some)]
    load_all(pairs, sems)
    pairs, at = [], 0
    for turn, some in enumerate(places):
        delta, own, others, done = scratch[4 * turn : 4 * turn + 4]
        span = delta.shape[2]
        for group, place in enumerate(some):
            columns = slice(group * span, (group + 1) * span)
            total = own[:, columns]
            for n in range(mp_count - 1):
                total = total + others[n, :, columns].astype(jnp.float32)
            done[:, columns] = (total + delta[group].astype(jnp.float32)).astype(done.dtype)
            target = pl.ds(pl.multiple_of(info_ref[place + 1] * span, span), span)
            pairs.append((done.at[rows:, columns], away.at[:, at : at + span]))
            pairs.append((done.at[:rows, columns], out.at[:, target]))
            at += span
    load_all(pairs, sems)


def finish(info, places, delta, parts, held, width, *before):
    mp_count, rows = len(parts[0]), parts[0][0].shape[0]
    span = delta.shape[2]
    count = sum(len(some) for some in places)
    operands = [info, delta, *sum(parts, []), *before] + ([] if held is None else [held])
    scratch = []
    for some in places:
        wide = span * len(some)
        scratch += [
            pltpu.VMEM((len(some), rows, span), delta.dtype),
            pltpu.VMEM((rows, wide), jnp.float32),
            pltpu.VMEM((mp_count - 1, rows, wide), delta.dtype),
            pltpu.VMEM((rows, wide), delta.dtype),
        ]
    held_bytes = rows * span * count * (2 * mp_count + 6)
    return pl.pallas_call(
        functools.partial(finish_kernel, mp_count, places),
        in_specs=[SCALARS] + [ANYWHERE] * (len(operands) - 1),
        out_specs=[ANYWHERE] * 2,
        out_shape=[
            jax.ShapeDtypeStruct((rows // CORES, width), delta.dtype),
            jax.ShapeDtypeStruct((rows // CORES, span * count), delta.dtype),
        ],
        scratch_shapes=scratch + [pltpu.SemaphoreType.DMA((mp_count * len(places) + 2 * count,))],
        input_output_aliases={} if held is None else {len(operands) - 1: 0},
        compiler_params=pltpu.CompilerParams(vmem_limit_bytes=VMEM_BYTES // 10 + held_bytes + held_bytes // 4),
        cost_estimate=cost(4 * rows * span * count, 12 * rows * span * count),
    )(*operands)


def settle_kernel(places, span, info_ref, *rest):
    pieces, (out, sems) = rest[: len(places)], rest[-2:]
    pairs = []
    for piece, some in zip(pieces, places):
        for group, place in enumerate(some):
            target = pl.ds(pl.multiple_of(info_ref[place] * span, span), span)
            pairs.append((piece.at[:, group * span : (group + 1) * span], out.at[:, target]))
    load_all(pairs, sems)


def settle(info, places, span, pieces, held):
    operands = [info, *pieces, held]
    return pl.pallas_call(
        functools.partial(settle_kernel, places, span),
        in_specs=[SCALARS] + [WHOLE] * len(pieces) + [ANYWHERE],
        out_specs=ANYWHERE,
        out_shape=jax.ShapeDtypeStruct(held.shape, held.dtype),
        scratch_shapes=[pltpu.SemaphoreType.DMA((sum(len(some) for some in places),))],
        input_output_aliases={len(operands) - 1: 0},
        compiler_params=pltpu.CompilerParams(vmem_limit_bytes=VMEM_BYTES // 6),
        cost_estimate=cost(0, 4 * sum(piece.size for piece in pieces)),
    )(*operands)


def by_plane(plane, values):
    return sum(jnp.where(plane == n, value, 0) for n, value in enumerate(values)).astype(jnp.int32)


def arrival_order(plane, planes):
    sides = (1, -1) if 2 * plane < planes else (-1, 1)
    return [
        (side, distance)
        for distance in range(1, planes)
        for side in sides
        if 0 <= plane + side * distance < planes
    ]


def local(tokens, frozen_weight, adapter_down_weight, adapter_up_weight, token_adapter_index):
    mp_count, dp_count = lax.axis_size("mp"), lax.axis_size("dp")
    position, replica = lax.axis_index("mp"), lax.axis_index("dp")
    planes = dp_count // CORES
    plane, core = replica // CORES, replica % CORES
    group_rows, features = tokens.shape
    rows = group_rows // mp_count
    width = frozen_weight.shape[1]
    adapters, rank, up_span = adapter_up_weight.shape[1:]
    ranks = adapters * rank

    def after_all(*arrays):
        return lax.optimization_barrier(arrays)

    def swap(array):
        return lax.ppermute(array, "dp", [(n, n ^ 1) for n in range(dp_count)])

    def trade(array):
        return lax.all_to_all(array, "mp", 0, 0)

    def pass_round(blocks):
        return [
            lax.ppermute(block, "mp", [(m, m ^ n) for m in range(mp_count)]) for n, block in enumerate(blocks, 1)
        ]

    def hop(array, side, step):
        sources = range(1, planes - step + 1) if side > 0 else range(step - 1, planes - 1)
        return lax.ppermute(
            array, "dp", [(CORES * n + m, CORES * (n - side) + m) for n in sources for m in range(CORES)]
        )

    got = {(side, 1): hop(frozen_weight, side, 1) for side in (1, -1)}
    other = swap(tokens)
    ids = token_adapter_index.reshape(group_rows, 1)
    ids = [ids, swap(token_adapter_index).reshape(group_rows, 1)]

    orders = [[(0, 0)] + arrival_order(n, planes) for n in range(planes)]
    options = [sorted({order[turn] for order in orders}) for turn in range(planes)]
    scalars = [position, core]
    choice_at, group_at = [], []
    for turn in range(planes):
        wanted = [order[turn] for order in orders]
        choice_at.append(len(scalars))
        scalars.append(by_plane(plane, [options[turn].index(item) for item in wanted]))
        group = by_plane(plane, [n + side * distance for n, (side, distance) in enumerate(wanted)])
        group_at.append(len(scalars))
        scalars += [group, CORES * group + core, CORES * group + 1 - core]
    info = jnp.stack([jnp.asarray(value, jnp.int32) for value in scalars])

    down = trade(cut_down(info, adapter_down_weight, mp_count))
    up = cut_up(info, adapter_up_weight.reshape(2, ranks, up_span), mp_count, width, down.shape[2])
    got[1, 1], got[-1, 1], up = after_all(got[1, 1], got[-1, 1], up)
    finished, places = [], []

    for turn in range(1, planes):
        last = turn == planes - 1
        if not last:
            if turn > 1:
                got[1, turn], got[-1, turn], own, sums = after_all(got[1, turn], got[-1, turn], own, sums)
            for side in (1, -1):
                got[side, turn + 1] = hop(got[side, turn], side, turn + 1)
        if turn > 1:
            finished.append([own] + pass_round(sent))
        before = []
        if last:
            delta = deltas_of(info, ids, sums, swap(sums), up, adapters, rank, planes, width)
            before = [delta]
        elif turn == 2:
            sums = trade(sums)
            up, sums = after_all(up, sums)
            up = trade(up)
            before = finished[0][1:]
        turns = [0, 1] if turn == 1 else [turn]
        groups = [[frozen_weight] if n == 0 else [got[option] for option in options[n]] for n in turns]
        kept = True
        cover = 1 if turn == 1 else COVER
        own, *sent = base_products(
            info, [choice_at[n] for n in turns], tokens, other, groups, mp_count, kept, cover, *before
        )
        places.append([group_at[n] for n in turns])
        if turn == 1:
            sums = low_sums(info, tokens, other, ids, down, adapters, rank, own)
    finished.append([own] + pass_round(sent))

    out, first = finish(info, places[:-1], delta, finished[:-1], None, dp_count * width, own)
    first = swap(first)
    out, second = finish(info, places[-1:], delta, finished[-1:], out, dp_count * width)
    second = swap(second)
    places = [place + 2 for some in places for place in some]
    out = settle(info, [places[:-1]], width, [first], out)
    return settle(info, [places[-1:]], width, [second], out)


def solution(mesh):
    placed = (P("dp", "mp"), P("mp", "dp"), P(None, "mp"), P(None, "mp", None, None), P("dp"))
    return jax.shard_map(
        local, mesh=mesh, in_specs=placed, out_specs=P(("dp", "mp"), None), check_vma=False
    )
```
